256 devices in a mesh: rows: 32 (over z, x), pairs: 8 (over y, core).
Axes of the slice: x: 4, y: 4, z: 8, core: 2. Of those that a mesh axis runs over, the one named last changes fastest.
Arguments:
- snapshot: float32 [32768, 8192], P('rows', 'pairs')
- plan: int32 [2, 8, 8], P(None, 'pairs'), may hold values from 0 to 7, each once within a row
Outputs:
- rotated: float32 [32768, 8192], P('rows', 'pairs')
The draws below stay inside these ranges and needn't reach their ends.
Inputs may be any that keep to these rules, and one draw needn't show every extreme that they name: Each plan[s, q, :] holds every local place exactly once.
All inputs are finite; a program needn't handle non-finite values.
Results may differ from the reference program's by a relative error of at most 0.0003.
Values sent between devices are 32-bit elements; how exact they have to be, the bound alone decides.
No kernel may reach another device: no remote copies, remote signals or barrier semaphores. Data moves between devices by JAX's collectives and lax.ppermute only.
A program may use at most 128 MiB of HBM per device.

```python
import jax
import jax.numpy as jnp
from jax import lax

BLK = 128
BLOCKS_DEV = 8
STEPS = 2
ROWS = 32768
COLS = 8192
N_PAIRS = 8


def draw_snapshot(key, part):
    key = jax.random.fold_in(key, 11)
    keys = jax.random.split(key, 5)
    position = jnp.arange(ROWS).astype(jnp.float32)
    rising = 1.0 + 2.0 * position / max(ROWS - 1, 1)
    noise = jax.random.normal(keys[0], (ROWS, COLS), jnp.float32)
    shared = jax.random.normal(keys[1], (ROWS, BLK), jnp.float32)
    common = jax.random.normal(keys[2], (ROWS, 16), jnp.float32)
    loading = jax.random.normal(keys[3], (16, COLS), jnp.float32)
    spread = jnp.exp(jax.random.uniform(keys[4], (ROWS,), jnp.float32, -0.3, 0.3))
    tiled = jnp.tile(shared, (1, COLS // BLK))
    ranked = jnp.zeros((ROWS, COLS), jnp.float32)
    for index in range(16):
        factor = 0.5 + 2.5 * index / 15.0
        ranked = ranked + common[:, index:index + 1] * (factor * loading[index:index + 1, :])
    values = noise + 0.8 * tiled + ranked
    return 0.12 * (rising * spread)[:, None] * values


def setup_inputs(seed: int = 0) -> dict:
    key_of = jax.random.split(jax.random.key(seed), 3)
    return {
        "snapshot": draw_snapshot(jax.random.fold_in(key_of[2], 71), 0),
        "plan": jax.vmap(lambda own: jax.random.permutation(own, BLOCKS_DEV))(jax.random.split(key_of[1], STEPS * N_PAIRS)).reshape((STEPS, N_PAIRS, BLOCKS_DEV)).astype(jnp.int32),
    }


def cayley_rotation(cross, norms, width):
    scale = lax.rsqrt(norms + 1e-06)
    half = 0.5 * cross * scale[:, :width, None] * scale[:, None, width:]
    count = cross.shape[0]
    zeros = jnp.zeros((count, width, width), jnp.float32)
    upper = jnp.concatenate([zeros, half], axis=2)
    lower = jnp.concatenate([-jnp.swapaxes(half, 1, 2), zeros], axis=2)
    skew = jnp.concatenate([upper, lower], axis=1)
    eye_big = jnp.eye(2 * width, dtype=jnp.float32)
    eye_small = jnp.eye(width, dtype=jnp.float32)
    hp = lax.Precision.HIGHEST
    square = eye_big + 2.0 * skew + jnp.einsum('pij,pjk->pik', skew, skew, precision=hp)
    first = eye_small + jnp.einsum('pij,pkj->pik', half, half, precision=hp)
    second = eye_small + jnp.einsum('pji,pjk->pik', half, half, precision=hp)

    def solve_block(spd, rhs):
        factor = jnp.linalg.cholesky(spd)
        return jax.scipy.linalg.cho_solve((factor, True), rhs)
    left_cols = jax.vmap(solve_block)(first, jnp.swapaxes(square[:, :, :width], 1, 2))
    right_cols = jax.vmap(solve_block)(second, jnp.swapaxes(square[:, :, width:], 1, 2))
    return jnp.concatenate([jnp.swapaxes(left_cols, 1, 2), jnp.swapaxes(right_cols, 1, 2)], axis=2)

def reference(snapshot, plan):
    hp = lax.Precision.HIGHEST
    blocks = snapshot.reshape(ROWS, N_PAIRS, BLOCKS_DEV, BLK)
    npair = N_PAIRS * (BLOCKS_DEV // 2)
    for step in range(STEPS):
        blocks = jax.vmap(lambda held, order: jnp.take(held, order, axis=1), in_axes=(1, 0), out_axes=1)(blocks, plan[step])
        paired = blocks.reshape(ROWS, npair, 2 * BLK)
        gram = jnp.einsum('rpi,rpj->pij', paired, paired, precision=hp)
        cross = gram[:, :BLK, BLK:]
        norms = jnp.diagonal(gram, axis1=1, axis2=2)
        rotation = cayley_rotation(cross, norms, BLK)
        turned = jnp.einsum('rpi,pij->rpj', paired, rotation, precision=hp)
        turned = turned.reshape(ROWS, N_PAIRS, BLOCKS_DEV // 2, 2, BLK)
        moved = jnp.roll(turned[:, :, :, 1], 1, axis=1)
        blocks = jnp.stack([turned[:, :, :, 0], moved], axis=3).reshape(ROWS, N_PAIRS, BLOCKS_DEV, BLK)
    return blocks.reshape(ROWS, COLS)
```

```python
import functools

import jax
import jax.numpy as jnp
from jax import lax
from jax.experimental import pallas as pl
from jax.experimental.pallas import tpu as pltpu
from jax.sharding import PartitionSpec as P

WIDTH = 128
PAIRS = 4
PANEL = 32
GROUP_ROWS = 136
HP = lax.Precision.HIGHEST
PARAMS = pltpu.CompilerParams(vmem_limit_bytes=48 * 1024 * 1024)


def split(value):
    high = value.astype(jnp.bfloat16)
    low = (value - high.astype(jnp.float32)).astype(jnp.bfloat16)
    return high, low


def dot3(left, right, dims):
    def one(a, b):
        return lax.dot_general(a, b, (dims, ((), ())), preferred_element_type=jnp.float32)

    return one(left[0], right[0]) + (one(left[0], right[1]) + one(left[1], right[0]))


def pick(plan_ref, place, sources, target, sem):
    block = plan_ref[place]
    if len(sources) == 1:
        start = pl.multiple_of(block * WIDTH, WIDTH)
        pltpu.make_async_copy(sources[0].at[:, pl.ds(start, WIDTH)], target, sem).start()
        return
    start = pl.multiple_of((block // 2) * WIDTH, WIDTH)
    for odd, source in enumerate(sources):

        @pl.when(block % 2 == odd)
        def _():
            pltpu.make_async_copy(source.at[:, pl.ds(start, WIDTH)], target, sem).start()


def picked(sources, target, sem):
    pltpu.make_async_copy(sources[0].at[:, pl.ds(0, WIDTH)], target, sem).wait()


def gram_kernel(nsrc, plan_ref, *refs):
    sources, (out_ref, held, sems) = refs[:nsrc], refs[nsrc:]
    for place in range(2 * PAIRS):
        pick(plan_ref, place, sources, held.at[place], sems.at[place])
    line = lax.broadcasted_iota(jnp.int32, (8, WIDTH), 0)
    for pair in range(PAIRS):
        for place in (2 * pair, 2 * pair + 1):
            picked(sources, held.at[place], sems.at[place])
        first, second = held[2 * pair], held[2 * pair + 1]
        out_ref[pair, :WIDTH, :] = lax.dot_general(
            first, second, (((0,), (0,)), ((), ())), precision=HP, preferred_element_type=jnp.float32
        )
        norm_first = jnp.sum(first * first, axis=0, keepdims=True)
        norm_second = jnp.sum(second * second, axis=0, keepdims=True)
        out_ref[pair, WIDTH:, :] = jnp.where(line == 0, norm_first, jnp.where(line == 1, norm_second, 0.0))


def gram(order, sources):
    height = sources[0].shape[0]
    return pl.pallas_call(
        functools.partial(gram_kernel, len(sources)),
        out_shape=jax.ShapeDtypeStruct((PAIRS, GROUP_ROWS, WIDTH), jnp.float32),
        in_specs=[pl.BlockSpec(memory_space=pltpu.SMEM)] + [pl.BlockSpec(memory_space=pl.ANY)] * len(sources),
        out_specs=pl.BlockSpec(memory_space=pltpu.VMEM),
        scratch_shapes=[
            pltpu.VMEM((2 * PAIRS, height, WIDTH), jnp.float32),
            pltpu.SemaphoreType.DMA((2 * PAIRS,)),
        ],
        compiler_params=PARAMS,
        name="gram",
    )(order, *sources)


def panel_inverse(block):
    row = lax.broadcasted_iota(jnp.int32, block.shape, 0)
    lane = lax.broadcasted_iota(jnp.int32, block.shape, 1)
    base = (lane // PANEL) * PANEL
    inner = lane - base
    for j in range(PANEL):
        column = jnp.take_along_axis(block, base + j, axis=1)
        inverse = 1.0 / column[j : j + 1, :]
        at_j = inner == j
        line = jnp.where(at_j[j : j + 1, :], inverse, block[j : j + 1, :] * inverse)
        block = jnp.where(row == j, line, jnp.where(at_j, 0.0, block) - column * line)
    return block


def rotations(sums, count):
    width = WIDTH
    row = lax.broadcasted_iota(jnp.int32, (width, width), 0)
    lane = lax.broadcasted_iota(jnp.int32, (width, width), 1)
    eye = (row == lane).astype(jnp.float32)
    halves, systems = [], []
    for pair in range(count):
        cross = sums[pair, :width, :]
        scale = lax.rsqrt(sums[pair, width:, :] + 1e-06)
        down = jnp.sum(eye * scale[0:1, :], axis=1, keepdims=True)
        half = 0.5 * cross * down * scale[1:2, :]
        spd = eye + lax.dot_general(half, half, (((1,), (1,)), ((), ())), precision=HP, preferred_element_type=jnp.float32)
        halves.append(half)
        systems.append((spd, half))
    group = lane // PANEL
    for panel in range(width // PANEL):
        lo, hi = panel * PANEL, (panel + 1) * PANEL
        packed = None
        for pair in range(count):
            part = systems[pair][0][lo:hi, :]
            shift = (pair * PANEL - lo) % width
            if shift:
                part = pltpu.roll(part, shift, 1)
            packed = part if packed is None else jnp.where(group[:PANEL] == pair, part, packed)
        inverse = panel_inverse(packed)
        spread = jnp.where(row // PANEL == group, jnp.concatenate([inverse] * PAIRS, axis=0), 0.0)
        in_panel = group[:PANEL] == panel
        tops = [jnp.where(in_panel, eye[lo:hi, :], systems[pair][0][lo:hi, :]) for pair in range(count)]
        fill = [jnp.zeros((PANEL, width), jnp.float32)] * (PAIRS - count)
        stacked = [
            jnp.concatenate(tops + fill, axis=0),
            jnp.concatenate([systems[pair][1][lo:hi, :] for pair in range(count)] + fill, axis=0),
        ]
        fresh = [jnp.dot(spread, side, precision=HP, preferred_element_type=jnp.float32) for side in stacked]
        row_in = row // PANEL == panel
        nothing_above = [jnp.zeros((lo, width), jnp.float32)] if lo else []
        nothing_below = [jnp.zeros((width - hi, width), jnp.float32)] if hi < width else []
        done = []
        for pair in range(count):
            spd, rest = systems[pair]
            sides = []
            for side, new in zip((jnp.where(group == panel, 0.0, spd), rest), fresh):
                mine = new[pair * PANEL : (pair + 1) * PANEL, :]
                placed = jnp.concatenate(nothing_above + [mine] + nothing_below, axis=0)
                change = jnp.dot(spd, placed, precision=HP, preferred_element_type=jnp.float32)
                sides.append(jnp.where(row_in, placed, side - change))
            done.append(tuple(sides))
        systems = done
    return [(halves[pair],) + systems[pair] for pair in range(count)]


def turn_kernel(nsrc, plan_ref, sums_ref, *refs):
    sources, (stay_ref, moved_ref, held, stay, moved, in_sems, out_sems) = refs[:nsrc], refs[nsrc:]
    for place in range(2 * PAIRS):
        pick(plan_ref, place, sources, held.at[place], in_sems.at[place])
    width = WIDTH
    row = lax.broadcasted_iota(jnp.int32, (width, width), 0)
    lane = lax.broadcasted_iota(jnp.int32, (width, width), 1)
    eye = (row == lane).astype(jnp.float32)
    solved = rotations(sums_ref, PAIRS)
    every = ((1,), (0,))
    copies = []
    stride = stay_ref.shape[1] // PAIRS
    for pair in range(PAIRS):
        half, inverse, across = solved[pair]
        top_left = 2.0 * inverse - eye
        top_right = 2.0 * across
        bottom_right = eye - 2.0 * lax.dot_general(
            half, across, (((0,), (0,)), ((), ())), precision=HP, preferred_element_type=jnp.float32
        )
        rotation = jnp.concatenate(
            [
                jnp.concatenate([top_left, top_right], axis=1),
                jnp.concatenate([-top_right.T, bottom_right], axis=1),
            ],
            axis=0,
        )
        for place in (2 * pair, 2 * pair + 1):
            picked(sources, held.at[place], in_sems.at[place])
        both = jnp.concatenate([held[2 * pair], held[2 * pair + 1]], axis=1)
        turned = dot3(split(both), split(rotation), every)
        stay[pair] = turned[:, :width]
        moved[pair] = turned[:, width:]
        copies.append(
            pltpu.make_async_copy(moved.at[pair], moved_ref.at[:, pl.ds(pair * width, width)], out_sems.at[2 * pair])
        )
        copies[-1].start()
        copies.append(
            pltpu.make_async_copy(stay.at[pair], stay_ref.at[:, pl.ds(pair * stride, width)], out_sems.at[2 * pair + 1])
        )
        copies[-1].start()
    for copy in copies:
        copy.wait()


def turn(order, sums, sources, last):
    height = sources[0].shape[0]
    across = PAIRS * WIDTH
    blocks = (PAIRS, height, WIDTH)
    return pl.pallas_call(
        functools.partial(turn_kernel, len(sources)),
        out_shape=(
            jax.ShapeDtypeStruct((height, 2 * across if last else across), jnp.float32),
            jax.ShapeDtypeStruct((height, across), jnp.float32),
        ),
        in_specs=[pl.BlockSpec(memory_space=pltpu.SMEM), pl.BlockSpec(memory_space=pltpu.VMEM)]
        + [pl.BlockSpec(memory_space=pl.ANY)] * len(sources),
        out_specs=[pl.BlockSpec(memory_space=pl.ANY)] * 2,
        scratch_shapes=[
            pltpu.VMEM((2 * PAIRS, height, WIDTH), jnp.float32),
            pltpu.VMEM(blocks, jnp.float32),
            pltpu.VMEM(blocks, jnp.float32),
            pltpu.SemaphoreType.DMA((2 * PAIRS,)),
            pltpu.SemaphoreType.DMA((2 * PAIRS,)),
        ],
        compiler_params=PARAMS,
        name="turn",
    )(order, sums, *sources)


def fill_kernel(moved_ref, _, out_ref, sems):
    copies = [
        pltpu.make_async_copy(
            moved_ref.at[:, pl.ds(pair * WIDTH, WIDTH)],
            out_ref.at[:, pl.ds((2 * pair + 1) * WIDTH, WIDTH)],
            sems.at[pair],
        )
        for pair in range(PAIRS)
    ]
    for copy in copies:
        copy.start()
    for copy in copies:
        copy.wait()


def fill(moved, out):
    return pl.pallas_call(
        fill_kernel,
        out_shape=jax.ShapeDtypeStruct(out.shape, out.dtype),
        in_specs=[pl.BlockSpec(memory_space=pl.ANY)] * 2,
        out_specs=pl.BlockSpec(memory_space=pl.ANY),
        scratch_shapes=[pltpu.SemaphoreType.DMA((PAIRS,))],
        input_output_aliases={1: 0},
        compiler_params=PARAMS,
        name="fill",
    )(moved, out)


def summed(parts, nx):
    count = lax.axis_size("rows")
    nz = count // nx
    beside = [[z * nx + x for x in range(nx)] for z in range(nz)]
    parts = lax.all_to_all(parts, "rows", 0, 0, axis_index_groups=beside)
    mine = jnp.sum(parts, axis=0)
    step = 1
    while step < nz:
        mine = mine + lax.ppermute(mine, "rows", [(i, (((i // nx) ^ step) * nx) + i % nx) for i in range(count)])
        step *= 2
    return lax.all_to_all(jnp.broadcast_to(mine, (nx,) + mine.shape), "rows", 0, 0, axis_index_groups=beside)


def local(snapshot, plan):
    count = lax.axis_size("pairs")
    onward = [(q, (q + 1) % count) for q in range(count)]
    sources = (snapshot,)
    steps = plan.shape[0]
    for step in range(steps):
        order = plan[step, 0]
        sums = summed(gram(order, sources), PAIRS)
        stay, moved = turn(order, sums, sources, step == steps - 1)
        sources = (stay, lax.ppermute(moved, "pairs", onward))
    return fill(sources[1], sources[0])


def solution(mesh):
    return jax.shard_map(
        local,
        mesh=mesh,
        in_specs=(P("rows", "pairs"), P(None, "pairs", None)),
        out_specs=P("rows", "pairs"),
        check_vma=False,
    )
```

```python
import functools

import jax
import jax.numpy as jnp
from jax import lax
from jax.experimental import pallas as pl
from jax.experimental.pallas import tpu as pltpu
from jax.sharding import PartitionSpec as P

WIDTH = 128
PAIRS = 4
PLACES = 2 * PAIRS
PANEL = 32
PACK = WIDTH // PANEL
SUB = 8
GROUP = 8
GROUP_ROWS = 136
HP = lax.Precision.HIGHEST
PARAMS = pltpu.CompilerParams(vmem_limit_bytes=48 * 1024 * 1024)


def split(value):
    high = value.astype(jnp.bfloat16)
    return high, (value - high.astype(jnp.float32)).astype(jnp.bfloat16)


def load_blocks(source, held, sems):
    for place in range(PLACES):
        pltpu.make_async_copy(source.at[:, pl.ds(place * WIDTH, WIDTH)], held.at[place], sems.at[place]).start()


def wait_block(source, held, sems, place):
    pltpu.make_async_copy(source.at[:, pl.ds(0, WIDTH)], held.at[place], sems.at[place]).wait()


def gram_kernel(step, x_ref, *refs):
    if step is None:
        out_ref, held, sems = refs
        load_blocks(x_ref, held, sems)
        order = list(range(PLACES))
    else:
        plan_ref, out_ref, held, sems, plan, plan_sem = refs
        load_plan = pltpu.make_async_copy(plan_ref, plan, plan_sem)
        load_plan.start()
        load_blocks(x_ref, held, sems)
        load_plan.wait()
        order = [plan[step, 0, place] for place in range(PLACES)]
    line = lax.broadcasted_iota(jnp.int32, (8, WIDTH), 0)
    for pair in range(PAIRS):
        both = order[2 * pair : 2 * pair + 2]
        for place in both:
            wait_block(x_ref, held, sems, place)
        first, second = held[both[0]], held[both[1]]
        out_ref[pair, :WIDTH, :] = lax.dot_general(
            first, second, (((0,), (0,)), ((), ())), precision=HP, preferred_element_type=jnp.float32
        )
        norm_first = jnp.sum(first * first, axis=0, keepdims=True)
        norm_second = jnp.sum(second * second, axis=0, keepdims=True)
        out_ref[pair, WIDTH:, :] = jnp.where(line == 0, norm_first, jnp.where(line == 1, norm_second, 0.0))


def gram(x, plan, step):
    planned = step is not None
    scratch = [pltpu.VMEM((PLACES, x.shape[0], WIDTH), jnp.float32), pltpu.SemaphoreType.DMA((PLACES,))]
    if planned:
        scratch += [pltpu.SMEM(plan.shape, jnp.int32), pltpu.SemaphoreType.DMA]
    return pl.pallas_call(
        functools.partial(gram_kernel, step),
        out_shape=jax.ShapeDtypeStruct((PAIRS, GROUP_ROWS, WIDTH), jnp.float32),
        in_specs=[pl.BlockSpec(memory_space=pl.ANY)] * (2 if planned else 1),
        out_specs=pl.BlockSpec(memory_space=pltpu.VMEM),
        scratch_shapes=scratch,
        compiler_params=PARAMS,
        name="gram",
    )(*((x, plan) if planned else (x,)))


def panel_inverse(block):
    parts = [block[i : i + SUB, :] for i in range(0, PANEL, SUB)]
    row = lax.broadcasted_iota(jnp.int32, (SUB, WIDTH), 0)
    lane = lax.broadcasted_iota(jnp.int32, (SUB, WIDTH), 1)
    base = (lane // PANEL) * PANEL
    inner = lane - base

    def line(value, j):
        return jnp.broadcast_to(value[j // SUB][j % SUB : j % SUB + 1, :], (SUB, WIDTH))

    def column(value, j):
        return [jnp.take_along_axis(part, base + j, axis=1) for part in value]

    for start in range(0, PANEL, GROUP):
        columns = [column(parts, j) for j in range(start, start + GROUP)]
        for j in range(start, start + GROUP, 2):
            c0, c1, *columns = columns
            a, b, d = line(c0, j), line(c1, j), line(c1, j + 1)
            r = 1.0 / (a * d - b * b)

            def update(value, u, v, cleared):
                m0, m1 = (d * u - b * v), (a * v - b * u)
                out = []
                for i in range(len(value)):
                    old = value[i] if cleared is None else jnp.where(cleared, 0.0, value[i])
                    out.append(old - (c0[i] * m0 + c1[i] * m1) * r)
                i = j // SUB
                out[i] = jnp.where(row == j % SUB, m0 * r, jnp.where(row == j % SUB + 1, m1 * r, out[i]))
                return out
            columns = [update(c, line(c, j), line(c, j + 1), None) for c in columns]
            at0, at1 = inner == j, inner == j + 1
            u = jnp.where(at0, 1.0, jnp.where(at1, 0.0, line(parts, j)))
            v = jnp.where(at1, 1.0, jnp.where(at0, 0.0, line(parts, j + 1)))
            parts = update(parts, u, v, at0 | at1)
    return jnp.concatenate(parts, axis=0)


def split3(value):
    high = value.astype(jnp.bfloat16)
    rest = value - high.astype(jnp.float32)
    middle = rest.astype(jnp.bfloat16)
    return high, middle, (rest - middle.astype(jnp.float32)).astype(jnp.bfloat16)


def contract(left, right, over):
    return lax.dot_general(left, right, (((over,), (over,)), ((), ())), preferred_element_type=jnp.float32)


def tall_dot(left, right):
    (a, b, c), (d, e, f) = left, right
    return contract(jnp.concatenate([a, b, a, b, c, a], axis=0), jnp.concatenate([d, d, e, e, d, f], axis=0), 0)


def square_dot(left, right, over):
    (a, b, c), (d, e, f) = left, right
    pair = lambda x, y: jnp.concatenate([x, y], axis=over)
    return contract(pair(a, b), pair(d, e), over) + (
        contract(pair(a, b), pair(e, d), over) + contract(pair(a, c), pair(f, d), over)
    )


def rotations(sums, count):
    width = WIDTH
    row = lax.broadcasted_iota(jnp.int32, (width, width), 0)
    lane = lax.broadcasted_iota(jnp.int32, (width, width), 1)
    eye = (row == lane).astype(jnp.float32)
    halves, systems = [], []
    for pair in range(count):
        cross = sums[pair][:width, :]
        scale = lax.rsqrt(sums[pair][width:, :] + 1e-06)
        down = jnp.sum(eye * scale[0:1, :], axis=1, keepdims=True)
        half = 0.5 * cross * down * scale[1:2, :]
        parts = split3(half)
        spd = eye + square_dot(parts, parts, 1)
        halves.append((half, parts))
        systems.append(jnp.concatenate([spd, half], axis=1))
    group = lax.broadcasted_iota(jnp.int32, (PANEL, width), 1) // PANEL
    wide = lax.broadcasted_iota(jnp.int32, (PANEL, 2 * width), 1)
    wide_row = lax.broadcasted_iota(jnp.int32, (PANEL, 2 * width), 0)
    for panel in range(width // PANEL):
        lo, hi = panel * PANEL, (panel + 1) * PANEL
        inside = (wide >= lo) & (wide < hi)
        cleared = jnp.concatenate([inside] * (width // PANEL), axis=0)
        done = []
        for first in range(0, count, PACK):
            members = range(first, min(first + PACK, count))
            packed = None
            for pair in members:
                part = systems[pair][lo:hi, :width]
                shift = ((pair - first) * PANEL - lo) % width
                if shift:
                    part = pltpu.roll(part, shift, 1)
                packed = part if packed is None else jnp.where(group == pair - first, part, packed)
            inverse = split3(panel_inverse(packed))
            for pair in members:
                old = systems[pair]
                top = old[lo:hi, :]
                unit = jnp.where(inside, (wide - lo == wide_row).astype(jnp.float32), top)
                at = (pair - first) * PANEL
                fresh = tall_dot(inverse, split3(unit))[at : at + PANEL, :]
                side = jnp.where(lane[:PANEL] < lo, -top[:, :width], top[:, :width])
                change = tall_dot(split3(side), split3(fresh))
                updated = jnp.where(cleared, 0.0, old) - change
                done.append(jnp.concatenate(([updated[:lo]] if lo else []) + [fresh] + ([updated[hi:]] if hi < width else []), axis=0))
        systems = done
    return [(halves[pair][0], systems[pair][:, :width], systems[pair][:, width:]) for pair in range(count)]


def turn_kernel(step, sums_ref, own_ref, prev_ref, *refs):
    if step is None:
        out_ref, held, sides, turned, in_sems, out_sems = refs
        plans = []
    else:
        own_plan_ref, prev_plan_ref, out_ref, held, sides, turned, in_sems, out_sems, plan, plan_sems = refs
        plans = [
            pltpu.make_async_copy(ref, plan.at[which], plan_sems.at[which])
            for which, ref in enumerate((own_plan_ref, prev_plan_ref))
        ]
        for copy in plans:
            copy.start()
    for which, ref in enumerate((own_ref, prev_ref)):
        load_blocks(ref, held.at[which], in_sems.at[which])
    width = WIDTH
    row = lax.broadcasted_iota(jnp.int32, (width, width), 0)
    lane = lax.broadcasted_iota(jnp.int32, (width, width), 1)
    eye = (row == lane).astype(jnp.float32)
    sums = [sums_ref.at[pair, which] for which in range(2) for pair in range(PAIRS)]
    for index, (half, inverse, across) in enumerate(rotations(sums, len(sums))):
        if index < PAIRS:
            top, bottom = 2.0 * inverse - eye, -2.0 * across.T
        else:
            top, bottom = 2.0 * across, eye - 2.0 * square_dot(split3(half), split3(across), 0)
        high, low = split(jnp.concatenate([top, bottom], axis=0))
        sides[index, :, :width] = high
        sides[index, :, width:] = low
    for copy in plans:
        copy.wait()
    for which, ref in enumerate((own_ref, prev_ref)):
        for place in range(PLACES):
            wait_block(ref, held.at[which], in_sems.at[which], place)
    copies = []
    for slot in range(PLACES):
        if step is None:
            which, pair = slot % 2, slot // 2
            first, second = 2 * pair, 2 * pair + 1
        else:
            place = plan[0, step + 1, 0, slot]
            which, pair = place % 2, place // 2
            first, second = plan[which, step, 0, 2 * pair], plan[which, step, 0, 2 * pair + 1]
        high, low = split(jnp.concatenate([held[which, first], held[which, second]], axis=1))
        side = sides[which * PAIRS + pair]
        parts = jnp.dot(high, side, preferred_element_type=jnp.float32)
        rest = jnp.dot(low, side[:, :width], preferred_element_type=jnp.float32)
        turned[slot] = parts[:, :width] + (parts[:, width:] + rest)
        copies.append(
            pltpu.make_async_copy(turned.at[slot], out_ref.at[:, pl.ds(slot * width, width)], out_sems.at[slot])
        )
        copies[-1].start()
    for copy in copies:
        copy.wait()


def turn(sums, own, prev, own_plan, prev_plan, step):
    planned = step is not None
    height = own.shape[0]
    scratch = [
        pltpu.VMEM((2, PLACES, height, WIDTH), jnp.float32),
        pltpu.VMEM((2 * PAIRS, 2 * WIDTH, 2 * WIDTH), jnp.bfloat16),
        pltpu.VMEM((PLACES, height, WIDTH), jnp.float32),
        pltpu.SemaphoreType.DMA((2, PLACES)),
        pltpu.SemaphoreType.DMA((PLACES,)),
    ]
    if planned:
        scratch += [pltpu.SMEM((2,) + own_plan.shape, jnp.int32), pltpu.SemaphoreType.DMA((2,))]
    return pl.pallas_call(
        functools.partial(turn_kernel, step),
        out_shape=jax.ShapeDtypeStruct(own.shape, jnp.float32),
        in_specs=[pl.BlockSpec(memory_space=pltpu.VMEM)] + [pl.BlockSpec(memory_space=pl.ANY)] * (4 if planned else 2),
        out_specs=pl.BlockSpec(memory_space=pl.ANY),
        scratch_shapes=scratch,
        compiler_params=PARAMS,
        name="turn",
    )(sums, own, prev, *((own_plan, prev_plan) if planned else ()))


def summed(parts, onward):
    nx, count = PAIRS, lax.axis_size("rows")
    nz = count // nx
    beside = [[z * nx + x for x in range(nx)] for z in range(nz)]
    parts = lax.all_to_all(parts, "rows", 0, 0, axis_index_groups=beside)
    mine = jnp.sum(parts, axis=0)
    step = 1
    while step < nz:
        mine = mine + lax.ppermute(mine, "rows", [(i, (((i // nx) ^ step) * nx) + i % nx) for i in range(count)])
        step *= 2
    both = jnp.stack([mine, lax.ppermute(mine, "pairs", onward)])
    return lax.all_to_all(jnp.broadcast_to(both, (nx,) + both.shape), "rows", 0, 0, axis_index_groups=beside)


def local(snapshot, plan):
    count = lax.axis_size("pairs")
    onward = [(q, (q + 1) % count) for q in range(count)]
    steps = plan.shape[0]
    prev_plan = lax.ppermute(plan, "pairs", onward)
    x = snapshot
    for step in range(steps):
        prev = lax.ppermute(x, "pairs", onward)
        sums = summed(gram(x, plan, step if step == 0 else None), onward)
        x = turn(sums, x, prev, plan, prev_plan, step if step == 0 else None)
    return x


def solution(mesh):
    return jax.shard_map(
        local,
        mesh=mesh,
        in_specs=(P("rows", "pairs"), P(None, "pairs", None)),
        out_specs=P("rows", "pairs"),
        check_vma=False,
    )
```

```python
import functools

import jax
import jax.numpy as jnp
from jax import lax
from jax.experimental import pallas as pl
from jax.experimental.pallas import tpu as pltpu
from jax.sharding import PartitionSpec as P

WIDTH = 128
PAIRS = 4
PLACES = 2 * PAIRS
EARLY = 5
PANEL = 32
PACK = WIDTH // PANEL
SUB = 8
GROUP = 8
GROUP_ROWS = 136
HP = lax.Precision.HIGHEST
PARAMS = pltpu.CompilerParams(vmem_limit_bytes=48 * 1024 * 1024)


def split(value):
    high = value.astype(jnp.bfloat16)
    return high, (value - high.astype(jnp.float32)).astype(jnp.bfloat16)


def blocks_of(arrays):
    return [
        array.at[:, pl.ds(start, WIDTH)] for array in arrays for start in range(0, array.shape[1], WIDTH)
    ]


def load_blocks(arrays, held, sems):
    for place, block in enumerate(blocks_of(arrays)):
        pltpu.make_async_copy(block, held.at[place], sems.at[place]).start()


def wait_blocks(arrays, held, sems):
    for place, block in enumerate(blocks_of(arrays)):
        pltpu.make_async_copy(block, held.at[place], sems.at[place]).wait()


def gram_blocks(held, order, out_ref):
    line = lax.broadcasted_iota(jnp.int32, (8, WIDTH), 0)
    for pair in range(PAIRS):
        first, second = held[order[2 * pair]], held[order[2 * pair + 1]]
        out_ref[pair, :WIDTH, :] = lax.dot_general(
            first, second, (((0,), (0,)), ((), ())), precision=HP, preferred_element_type=jnp.float32
        )
        norm_first = jnp.sum(first * first, axis=0, keepdims=True)
        norm_second = jnp.sum(second * second, axis=0, keepdims=True)
        out_ref[pair, WIDTH:, :] = jnp.where(line == 0, norm_first, jnp.where(line == 1, norm_second, 0.0))


def first_gram_kernel(plan_ref, x_ref, out_ref, early_ref, late_ref, held, sems, out_sems, plan, plan_sem):
    load_plan = pltpu.make_async_copy(plan_ref, plan, plan_sem)
    load_plan.start()
    load_blocks((x_ref,), held, sems)
    wait_blocks((x_ref,), held, sems)
    copies = [
        pltpu.make_async_copy(held.at[place], block, out_sems.at[place])
        for place, block in enumerate(blocks_of((early_ref, late_ref)))
    ]
    for copy in copies:
        copy.start()
    load_plan.wait()
    gram_blocks(held, [plan[0, 0, place] for place in range(PLACES)], out_ref)
    for copy in copies:
        copy.wait()


def later_gram_kernel(early_ref, late_ref, out_ref, held, sems):
    load_blocks((early_ref, late_ref), held, sems)
    wait_blocks((early_ref, late_ref), held, sems)
    gram_blocks(held, range(PLACES), out_ref)


SUMS = jax.ShapeDtypeStruct((PAIRS, GROUP_ROWS, WIDTH), jnp.float32)


def pieces(height):
    return tuple(jax.ShapeDtypeStruct((height, count * WIDTH), jnp.float32) for count in (EARLY, PLACES - EARLY))


def first_gram(x, plan):
    height = x.shape[0]
    return pl.pallas_call(
        first_gram_kernel,
        out_shape=(SUMS,) + pieces(height),
        in_specs=[pl.BlockSpec(memory_space=pl.ANY), pl.BlockSpec(memory_space=pltpu.HBM)],
        out_specs=[pl.BlockSpec(memory_space=pltpu.VMEM)] + [pl.BlockSpec(memory_space=pltpu.HBM)] * 2,
        scratch_shapes=[
            pltpu.VMEM((PLACES, height, WIDTH), jnp.float32),
            pltpu.SemaphoreType.DMA((PLACES,)),
            pltpu.SemaphoreType.DMA((PLACES,)),
            pltpu.SMEM(plan.shape, jnp.int32),
            pltpu.SemaphoreType.DMA,
        ],
        compiler_params=PARAMS,
        name="first_gram",
    )(plan, x)


def later_gram(early, late):
    return pl.pallas_call(
        later_gram_kernel,
        out_shape=SUMS,
        in_specs=[pl.BlockSpec(memory_space=pltpu.HBM)] * 2,
        out_specs=pl.BlockSpec(memory_space=pltpu.VMEM),
        scratch_shapes=[
            pltpu.VMEM((PLACES, early.shape[0], WIDTH), jnp.float32),
            pltpu.SemaphoreType.DMA((PLACES,)),
        ],
        compiler_params=PARAMS,
        name="later_gram",
    )(early, late)


def panel_inverse(block):
    parts = [block[i : i + SUB, :] for i in range(0, PANEL, SUB)]
    row = lax.broadcasted_iota(jnp.int32, (SUB, WIDTH), 0)
    lane = lax.broadcasted_iota(jnp.int32, (SUB, WIDTH), 1)
    base = (lane // PANEL) * PANEL
    inner = lane - base

    def line(value, j):
        return jnp.broadcast_to(value[j // SUB][j % SUB : j % SUB + 1, :], (SUB, WIDTH))

    def column(value, j):
        return [jnp.take_along_axis(part, base + j, axis=1) for part in value]

    for start in range(0, PANEL, GROUP):
        columns = [column(parts, j) for j in range(start, start + GROUP)]
        for j in range(start, start + GROUP, 2):
            c0, c1, *columns = columns
            a, b, d = line(c0, j), line(c1, j), line(c1, j + 1)
            r = 1.0 / (a * d - b * b)

            def update(value, u, v, cleared):
                m0, m1 = (d * u - b * v), (a * v - b * u)
                out = []
                for i in range(len(value)):
                    old = value[i] if cleared is None else jnp.where(cleared, 0.0, value[i])
                    out.append(old - (c0[i] * m0 + c1[i] * m1) * r)
                i = j // SUB
                out[i] = jnp.where(row == j % SUB, m0 * r, jnp.where(row == j % SUB + 1, m1 * r, out[i]))
                return out
            columns = [update(c, line(c, j), line(c, j + 1), None) for c in columns]
            at0, at1 = inner == j, inner == j + 1
            u = jnp.where(at0, 1.0, jnp.where(at1, 0.0, line(parts, j)))
            v = jnp.where(at1, 1.0, jnp.where(at0, 0.0, line(parts, j + 1)))
            parts = update(parts, u, v, at0 | at1)
    return jnp.concatenate(parts, axis=0)


def split3(value):
    high = value.astype(jnp.bfloat16)
    rest = value - high.astype(jnp.float32)
    middle = rest.astype(jnp.bfloat16)
    return high, middle, (rest - middle.astype(jnp.float32)).astype(jnp.bfloat16)


def contract(left, right, over):
    return lax.dot_general(left, right, (((over,), (over,)), ((), ())), preferred_element_type=jnp.float32)


def tall_dot(left, right):
    (a, b, c), (d, e, f) = left, right
    return contract(jnp.concatenate([a, b, a, b, c, a], axis=0), jnp.concatenate([d, d, e, e, d, f], axis=0), 0)


def square_dot(left, right, over):
    (a, b, c), (d, e, f) = left, right
    pair = lambda x, y: jnp.concatenate([x, y], axis=over)
    return contract(pair(a, b), pair(d, e), over) + (
        contract(pair(a, b), pair(e, d), over) + contract(pair(a, c), pair(f, d), over)
    )


def rotations(sums, count):
    width = WIDTH
    row = lax.broadcasted_iota(jnp.int32, (width, width), 0)
    lane = lax.broadcasted_iota(jnp.int32, (width, width), 1)
    eye = (row == lane).astype(jnp.float32)
    halves, systems = [], []
    for pair in range(count):
        cross = sums[pair][:width, :]
        scale = lax.rsqrt(sums[pair][width:, :] + 1e-06)
        down = jnp.sum(eye * scale[0:1, :], axis=1, keepdims=True)
        half = 0.5 * cross * down * scale[1:2, :]
        parts = split3(half)
        spd = eye + square_dot(parts, parts, 1)
        halves.append((half, parts))
        systems.append(jnp.concatenate([spd, half], axis=1))
    group = lax.broadcasted_iota(jnp.int32, (PANEL, width), 1) // PANEL
    wide = lax.broadcasted_iota(jnp.int32, (PANEL, 2 * width), 1)
    wide_row = lax.broadcasted_iota(jnp.int32, (PANEL, 2 * width), 0)
    for panel in range(width // PANEL):
        lo, hi = panel * PANEL, (panel + 1) * PANEL
        inside = (wide >= lo) & (wide < hi)
        cleared = jnp.concatenate([inside] * (width // PANEL), axis=0)
        done = []
        for first in range(0, count, PACK):
            members = range(first, min(first + PACK, count))
            packed = None
            for pair in members:
                part = systems[pair][lo:hi, :width]
                shift = ((pair - first) * PANEL - lo) % width
                if shift:
                    part = pltpu.roll(part, shift, 1)
                packed = part if packed is None else jnp.where(group == pair - first, part, packed)
            inverse = split3(panel_inverse(packed))
            for pair in members:
                old = systems[pair]
                top = old[lo:hi, :]
                unit = jnp.where(inside, (wide - lo == wide_row).astype(jnp.float32), top)
                at = (pair - first) * PANEL
                fresh = tall_dot(inverse, split3(unit))[at : at + PANEL, :]
                side = jnp.where(lane[:PANEL] < lo, -top[:, :width], top[:, :width])
                change = tall_dot(split3(side), split3(fresh))
                updated = jnp.where(cleared, 0.0, old) - change
                done.append(jnp.concatenate(([updated[:lo]] if lo else []) + [fresh] + ([updated[hi:]] if hi < width else []), axis=0))
        systems = done
    return [(halves[pair][0], systems[pair][:, :width], systems[pair][:, width:]) for pair in range(count)]


def rotate_kernel(sums_ref, sides_ref):
    width = WIDTH
    row = lax.broadcasted_iota(jnp.int32, (width, width), 0)
    lane = lax.broadcasted_iota(jnp.int32, (width, width), 1)
    eye = (row == lane).astype(jnp.float32)
    sums = [sums_ref.at[pair, which] for which in range(2) for pair in range(PAIRS)]
    for index, (half, inverse, across) in enumerate(rotations(sums, len(sums))):
        if index < PAIRS:
            top, bottom = 2.0 * inverse - eye, -2.0 * across.T
        else:
            top, bottom = 2.0 * across, eye - 2.0 * square_dot(split3(half), split3(across), 0)
        for start, part in ((0, top), (width, bottom)):
            high, low = split(part)
            sides_ref[index, start : start + width, :width] = high
            sides_ref[index, start : start + width, width:] = low


def rotate(sums):
    return pl.pallas_call(
        rotate_kernel,
        out_shape=jax.ShapeDtypeStruct((2 * PAIRS, 2 * WIDTH, 2 * WIDTH), jnp.bfloat16),
        in_specs=[pl.BlockSpec(memory_space=pltpu.VMEM)],
        out_specs=pl.BlockSpec(memory_space=pltpu.VMEM),
        compiler_params=PARAMS,
        name="rotate",
    )(sums)


def turn_kernel(last, sides_ref, early_ref, late_ref, prev_early_ref, prev_late_ref, *refs):
    if last:
        out_ref, held, turned, in_sems, out_sems = refs
        outs = (out_ref,)
        plans = []
    else:
        own_plan_ref, prev_plan_ref, *outs, held, turned, in_sems, out_sems, plan, plan_sems = refs
        plans = [
            pltpu.make_async_copy(ref, plan.at[which], plan_sems.at[which])
            for which, ref in enumerate((own_plan_ref, prev_plan_ref))
        ]
        for copy in plans:
            copy.start()
    sources = [blocks_of(arrays) for arrays in ((early_ref, late_ref), (prev_early_ref, prev_late_ref))]
    for place in range(PLACES):
        for which in range(2):
            pltpu.make_async_copy(sources[which][place], held.at[which, place], in_sems.at[which, place]).start()
    for copy in plans:
        copy.wait()
    width = WIDTH
    copies = []
    for slot, target in enumerate(blocks_of(outs)):
        if last:
            which, pair = slot % 2, slot // 2
            both = (2 * pair, 2 * pair + 1)
        else:
            place = plan[0, 1, 0, slot]
            which, pair = place % 2, place // 2
            both = (plan[which, 0, 0, 2 * pair], plan[which, 0, 0, 2 * pair + 1])
        for place in both:
            pltpu.make_async_copy(sources[0][0], held.at[which, place], in_sems.at[which, place]).wait()
        high, low = split(jnp.concatenate([held[which, place] for place in both], axis=1))
        side = sides_ref[which * PAIRS + pair]
        parts = jnp.dot(high, side, preferred_element_type=jnp.float32)
        rest = jnp.dot(low, side[:, :width], preferred_element_type=jnp.float32)
        turned[slot] = parts[:, :width] + (parts[:, width:] + rest)
        copies.append(pltpu.make_async_copy(turned.at[slot], target, out_sems.at[slot]))
        copies[-1].start()
    for copy in copies:
        copy.wait()


def turn(sides, own, prev, plans):
    height = own[0].shape[0]
    scratch = [
        pltpu.VMEM((2, PLACES, height, WIDTH), jnp.float32),
        pltpu.VMEM((PLACES, height, WIDTH), jnp.float32),
        pltpu.SemaphoreType.DMA((2, PLACES)),
        pltpu.SemaphoreType.DMA((PLACES,)),
    ]
    if plans:
        scratch += [pltpu.SMEM((2,) + plans[0].shape, jnp.int32), pltpu.SemaphoreType.DMA((2,))]
        shapes = pieces(height)
    else:
        shapes = (jax.ShapeDtypeStruct((height, PLACES * WIDTH), jnp.float32),)
    return pl.pallas_call(
        functools.partial(turn_kernel, not plans),
        out_shape=shapes,
        in_specs=[pl.BlockSpec(memory_space=pltpu.VMEM)]
        + [pl.BlockSpec(memory_space=pltpu.HBM)] * 4
        + [pl.BlockSpec(memory_space=pl.ANY)] * len(plans),
        out_specs=[pl.BlockSpec(memory_space=pltpu.HBM)] * len(shapes),
        scratch_shapes=scratch,
        compiler_params=PARAMS,
        name="turn",
    )(sides, *own, *prev, *plans)


def summed(parts, late, extra):
    nx, count = PAIRS, lax.axis_size("rows")
    nz = count // nx
    beside = [[z * nx + x for x in range(nx)] for z in range(nz)]
    parts = lax.all_to_all(parts, "rows", 0, 0, axis_index_groups=beside)
    mine = jnp.sum(parts, axis=0)
    step = 1
    while step < nz:
        turned = nz - 1 if 2 * step == nz else step
        mine = mine + lax.ppermute(mine, "rows", [(i, (((i // nx) ^ turned) * nx) + i % nx) for i in range(count)])
        step *= 2
    theirs, extra, late = lax.optimization_barrier((onward(mine), onward(extra) if extra is not None else (), late))
    late = onward(late)
    both = jnp.stack([mine, theirs])
    both = lax.all_to_all(jnp.broadcast_to(both, (nx,) + both.shape), "rows", 0, 0, axis_index_groups=beside)
    return both, late, extra


def onward(value):
    count = lax.axis_size("pairs")
    return lax.ppermute(value, "pairs", [(q, (q + 1) % count) for q in range(count)])


def local(snapshot, plan):
    parts, early, late = first_gram(snapshot, plan)
    prev_early = onward(early)
    sums, prev_late, prev_plan = summed(parts, late, plan)
    early, late = turn(rotate(sums), (early, late), (prev_early, prev_late), (plan, prev_plan))
    prev_early = onward(early)
    sums, prev_late, _ = summed(later_gram(early, late), late, None)
    return turn(rotate(sums), (early, late), (prev_early, prev_late), ())[0]


def solution(mesh):
    return jax.shard_map(
        local,
        mesh=mesh,
        in_specs=(P("rows", "pairs"), P(None, "pairs", None)),
        out_specs=P("rows", "pairs"),
        check_vma=False,
    )
```

```python
import functools

import jax
import jax.numpy as jnp
from jax import lax
from jax.experimental import pallas as pl
from jax.experimental.pallas import tpu as pltpu
from jax.sharding import PartitionSpec as P

WIDTH = 128
PAIRS = 4
PLACES = 2 * PAIRS
EARLY = 5
PANEL = 32
PACK = WIDTH // PANEL
SUB = 8
GROUP = 8
GROUP_ROWS = 136
HP = lax.Precision.HIGHEST
PARAMS = pltpu.CompilerParams(vmem_limit_bytes=28 * 1024 * 1024)


def split(value):
    high = value.astype(jnp.bfloat16)
    return high, (value - high.astype(jnp.float32)).astype(jnp.bfloat16)


def column_block(array, place):
    return array.at[:, pl.ds(place * WIDTH, WIDTH)]


def gram_pair(first, second, out_ref):
    a, b, c = split3(first)
    d, e, f = split3(second)
    large = contract(jnp.concatenate([a, b], axis=1), jnp.concatenate([d, e], axis=1), 0)
    small = contract(a, f, 0) + contract(c, d, 0)
    middle = large[:WIDTH, WIDTH:] + large[WIDTH:, :WIDTH]
    out_ref[:WIDTH, :] = large[:WIDTH, :WIDTH] + (middle + (large[WIDTH:, WIDTH:] + small))
    line = lax.broadcasted_iota(jnp.int32, (GROUP_ROWS - WIDTH, WIDTH), 0)
    norms = [jnp.sum(block * block, axis=0, keepdims=True) for block in (first, second)]
    out_ref[WIDTH:, :] = jnp.where(line == 0, norms[0], jnp.where(line == 1, norms[1], 0.0))


def first_gram_kernel(plan_ref, x_ref, gram_ref, early_ref, late_ref, held, sems, out_sems, plan, plan_sem):
    load_plan = pltpu.make_async_copy(plan_ref, plan, plan_sem)
    load_plan.start()
    loads = [
        pltpu.make_async_copy(column_block(x_ref, place), held.at[place], sems.at[place]) for place in range(PLACES)
    ]
    for copy in loads:
        copy.start()
    copies = []
    for place in range(PLACES):
        loads[place].wait()
        target = early_ref.at[place] if place < EARLY else late_ref.at[place - EARLY]
        copies.append(pltpu.make_async_copy(held.at[place], target, out_sems.at[place]))
        copies[-1].start()
    load_plan.wait()
    for pair in range(PAIRS):
        gram_pair(held[plan[0, 0, 2 * pair]], held[plan[0, 0, 2 * pair + 1]], gram_ref.at[pair])
    for copy in copies:
        copy.wait()


SUMS = jax.ShapeDtypeStruct((PAIRS, GROUP_ROWS, WIDTH), jnp.float32)


def blocks(count, height):
    return pltpu.HBM((count, height, WIDTH), jnp.float32)


def in_hbm(*arrays):
    return tuple(pltpu.with_memory_space_constraint(array, pltpu.HBM) for array in arrays)


def specs(*spaces):
    return [pl.BlockSpec(memory_space=space) for space in spaces]


def first_gram(x, plan):
    height = x.shape[0]
    return pl.pallas_call(
        first_gram_kernel,
        out_shape=(SUMS, blocks(EARLY, height), blocks(PLACES - EARLY, height)),
        in_specs=specs(pltpu.HBM, pltpu.HBM),
        out_specs=specs(pltpu.VMEM, pltpu.HBM, pltpu.HBM),
        scratch_shapes=[
            pltpu.VMEM((PLACES, height, WIDTH), jnp.float32),
            pltpu.SemaphoreType.DMA((PLACES,)),
            pltpu.SemaphoreType.DMA((PLACES,)),
            pltpu.SMEM(plan.shape, jnp.int32),
            pltpu.SemaphoreType.DMA,
        ],
        compiler_params=PARAMS,
        name="first_gram",
    )(*in_hbm(plan, x))


def panel_inverse(block):
    parts = [block[i : i + SUB, :] for i in range(0, PANEL, SUB)]
    row = lax.broadcasted_iota(jnp.int32, (SUB, WIDTH), 0)
    lane = lax.broadcasted_iota(jnp.int32, (SUB, WIDTH), 1)
    base = (lane // PANEL) * PANEL
    inner = lane - base

    def line(value, j):
        return jnp.broadcast_to(value[j // SUB][j % SUB : j % SUB + 1, :], (SUB, WIDTH))

    def column(value, j):
        return [jnp.take_along_axis(part, base + j, axis=1) for part in value]

    for start in range(0, PANEL, GROUP):
        columns = [column(parts, j) for j in range(start, start + GROUP)]
        for j in range(start, start + GROUP, 2):
            c0, c1, *columns = columns
            a, b, d = line(c0, j), line(c1, j), line(c1, j + 1)
            r = 1.0 / (a * d - b * b)

            def update(value, u, v, cleared):
                m0, m1 = (d * u - b * v), (a * v - b * u)
                out = []
                for i in range(len(value)):
                    old = value[i] if cleared is None else jnp.where(cleared, 0.0, value[i])
                    out.append(old - (c0[i] * m0 + c1[i] * m1) * r)
                i = j // SUB
                out[i] = jnp.where(row == j % SUB, m0 * r, jnp.where(row == j % SUB + 1, m1 * r, out[i]))
                return out
            columns = [update(c, line(c, j), line(c, j + 1), None) for c in columns]
            at0, at1 = inner == j, inner == j + 1
            u = jnp.where(at0, 1.0, jnp.where(at1, 0.0, line(parts, j)))
            v = jnp.where(at1, 1.0, jnp.where(at0, 0.0, line(parts, j + 1)))
            parts = update(parts, u, v, at0 | at1)
    return jnp.concatenate(parts, axis=0)


def split3(value):
    high = value.astype(jnp.bfloat16)
    rest = value - high.astype(jnp.float32)
    middle = rest.astype(jnp.bfloat16)
    return high, middle, (rest - middle.astype(jnp.float32)).astype(jnp.bfloat16)


def contract(left, right, over):
    return lax.dot_general(left, right, (((over,), (over,)), ((), ())), preferred_element_type=jnp.float32)


def tall_dot(left, right):
    (a, b, c), (d, e, f) = left, right
    return contract(jnp.concatenate([a, b, a, b, c, a], axis=0), jnp.concatenate([d, d, e, e, d, f], axis=0), 0)


def square_dot(left, right, over):
    (a, b, c), (d, e, f) = left, right
    pair = lambda x, y: jnp.concatenate([x, y], axis=over)
    return contract(pair(a, b), pair(d, e), over) + (
        contract(pair(a, b), pair(e, d), over) + contract(pair(a, c), pair(f, d), over)
    )


def rotations(sums, count):
    width = WIDTH
    row = lax.broadcasted_iota(jnp.int32, (width, width), 0)
    lane = lax.broadcasted_iota(jnp.int32, (width, width), 1)
    eye = (row == lane).astype(jnp.float32)
    halves, systems = [], []
    for pair in range(count):
        cross = sums[pair][:width, :]
        scale = lax.rsqrt(sums[pair][width:, :] + 1e-06)
        down = jnp.sum(eye * scale[0:1, :], axis=1, keepdims=True)
        half = 0.5 * cross * down * scale[1:2, :]
        parts = split3(half)
        spd = eye + square_dot(parts, parts, 1)
        halves.append((half, parts))
        systems.append(jnp.concatenate([spd, half], axis=1))
    group = lax.broadcasted_iota(jnp.int32, (PANEL, width), 1) // PANEL
    wide = lax.broadcasted_iota(jnp.int32, (PANEL, 2 * width), 1)
    wide_row = lax.broadcasted_iota(jnp.int32, (PANEL, 2 * width), 0)
    for panel in range(width // PANEL):
        lo, hi = panel * PANEL, (panel + 1) * PANEL
        inside = (wide >= lo) & (wide < hi)
        cleared = jnp.concatenate([inside] * (width // PANEL), axis=0)
        done = []
        for first in range(0, count, PACK):
            members = range(first, min(first + PACK, count))
            packed = None
            for pair in members:
                part = systems[pair][lo:hi, :width]
                shift = ((pair - first) * PANEL - lo) % width
                if shift:
                    part = pltpu.roll(part, shift, 1)
                packed = part if packed is None else jnp.where(group == pair - first, part, packed)
            inverse = split3(panel_inverse(packed))
            for pair in members:
                old = systems[pair]
                top = old[lo:hi, :]
                unit = jnp.where(inside, (wide - lo == wide_row).astype(jnp.float32), top)
                at = (pair - first) * PANEL
                fresh = tall_dot(inverse, split3(unit))[at : at + PANEL, :]
                side = jnp.where(lane[:PANEL] < lo, -top[:, :width], top[:, :width])
                change = tall_dot(split3(side), split3(fresh))
                updated = jnp.where(cleared, 0.0, old) - change
                done.append(jnp.concatenate(([updated[:lo]] if lo else []) + [fresh] + ([updated[hi:]] if hi < width else []), axis=0))
        systems = done
    return [(halves[pair][0], systems[pair][:, :width], systems[pair][:, width:]) for pair in range(count)]


def write_sides(sums_ref, sides_ref):
    width = WIDTH
    row = lax.broadcasted_iota(jnp.int32, (width, width), 0)
    lane = lax.broadcasted_iota(jnp.int32, (width, width), 1)
    eye = (row == lane).astype(jnp.float32)
    sums = [sums_ref.at[pair, which] for which in range(2) for pair in range(PAIRS)]

    def write(index, top, bottom):
        for start, part in ((0, top), (width, bottom)):
            high, low = split(part)
            sides_ref[index, start : start + width, :width] = high
            sides_ref[index, start : start + width, width:] = low

    for index, (half, inverse, across) in enumerate(rotations(sums, len(sums))):
        if index >= PAIRS:
            write(index, 2.0 * across, eye - 2.0 * square_dot(split3(half), split3(across), 0))
        left = index if index < PAIRS else index + PAIRS
        if left < sides_ref.shape[0]:
            write(left, 2.0 * inverse - eye, -2.0 * across.T)


def rotate_kernel(sums_ref, early_ref, late_ref, sides_ref, own_ref, sems):
    start_loads(sent_blocks(early_ref, late_ref), own_ref, sems)
    write_sides(sums_ref, sides_ref)
    wait_loads(own_ref, sems, range(PLACES))


def rotate(sums, own):
    return pl.pallas_call(
        rotate_kernel,
        out_shape=(
            jax.ShapeDtypeStruct((3 * PAIRS, 2 * WIDTH, 2 * WIDTH), jnp.bfloat16),
            pltpu.VMEM((PLACES, own[0].shape[1], WIDTH), jnp.float32),
        ),
        in_specs=specs(pltpu.VMEM, pltpu.HBM, pltpu.HBM),
        out_specs=specs(pltpu.VMEM, pltpu.VMEM),
        scratch_shapes=[pltpu.SemaphoreType.DMA((PLACES,))],
        compiler_params=PARAMS,
        name="rotate",
    )(sums, *in_hbm(*own))


def turned_pair(held, both, side):
    high, low = split(jnp.concatenate([held[place] for place in both], axis=1))
    parts = jnp.dot(high, side, preferred_element_type=jnp.float32)
    rest = jnp.dot(low, side[:, :WIDTH], preferred_element_type=jnp.float32)
    return parts[:, :WIDTH] + (parts[:, WIDTH:] + rest)


def start_loads(sources, held, sems):
    for place, source in enumerate(sources):
        pltpu.make_async_copy(source, held.at[place], sems.at[place]).start()


def wait_loads(held, sems, both):
    for place in both:
        pltpu.make_async_copy(held.at[0], held.at[place], sems.at[place]).wait()


def load_plans(refs, plan, sems):
    copies = [pltpu.make_async_copy(ref, plan.at[which], sems.at[which]) for which, ref in enumerate(refs)]
    for copy in copies:
        copy.start()
    return copies


def sent_blocks(early_ref, late_ref):
    return [early_ref.at[place] if place < EARLY else late_ref.at[place - EARLY] for place in range(PLACES)]


def both_of(plan, which, step, pair):
    return [plan[which, step, 0, 2 * pair + i] for i in range(2)]


def turn_all(step, own, prev, prev_sems, sides_ref, turned, outs, out_sems, plan):
    copies = []
    for which, held in enumerate((own, prev)):
        for pair in range(PAIRS):
            both = both_of(plan, which, step, pair)
            if which:
                wait_loads(prev, prev_sems, both)
            place = 2 * pair + which
            turned[place] = turned_pair(held, both, sides_ref[which * PAIRS + pair])
            target = column_block(outs[0], place) if len(outs) == 1 else outs[which].at[pair]
            copies.append(pltpu.make_async_copy(turned.at[place], target, out_sems.at[place]))
            copies[-1].start()
    return copies


def first_turn_kernel(
    sides_ref, own_ref, early_ref, late_ref, own_plan_ref, prev_plan_ref,
    gram_ref, stay_ref, moved_ref, held, turned, in_sems, out_sems, plan, plan_sems,
):
    plans = load_plans((own_plan_ref, prev_plan_ref), plan, plan_sems)
    start_loads(sent_blocks(early_ref, late_ref), held, in_sems)
    for copy in plans:
        copy.wait()
    copies = turn_all(0, own_ref, held, in_sems, sides_ref, turned, (stay_ref, moved_ref), out_sems, plan)
    for pair in range(PAIRS):
        first, second = [turned[place] for place in both_of(plan, 0, 1, pair)]
        gram_pair(first, second, gram_ref.at[pair])
    for copy in copies:
        copy.wait()


def first_turn(sides, own, prev, plans):
    height = own.shape[1]
    return pl.pallas_call(
        first_turn_kernel,
        out_shape=(SUMS, blocks(PAIRS, height), blocks(PAIRS, height)),
        in_specs=specs(pltpu.VMEM, pltpu.VMEM, *[pl.ANY] * 4),
        out_specs=specs(pltpu.VMEM, pltpu.HBM, pltpu.HBM),
        scratch_shapes=[
            pltpu.VMEM((PLACES, height, WIDTH), jnp.float32),
            pltpu.VMEM((PLACES, height, WIDTH), jnp.float32),
            pltpu.SemaphoreType.DMA((PLACES,)),
            pltpu.SemaphoreType.DMA((PLACES,)),
            pltpu.SMEM((2,) + plans[0].shape, jnp.int32),
            pltpu.SemaphoreType.DMA((2,)),
        ],
        compiler_params=PARAMS,
        name="first_turn",
    )(sides, own, *prev, *plans)


def prev_stay_kernel(sides_ref, early_ref, late_ref, plan_ref, out_ref, turned, out_sems, held, in_sems, plan, plan_sem):
    load_plan = pltpu.make_async_copy(plan_ref, plan.at[0], plan_sem)
    load_plan.start()
    start_loads(sent_blocks(early_ref, late_ref), held, in_sems)
    load_plan.wait()
    copies = []
    for pair in range(PAIRS):
        both = both_of(plan, 0, 0, pair)
        wait_loads(held, in_sems, both)
        turned[pair] = turned_pair(held, both, sides_ref[2 * PAIRS + pair])
        copies.append(pltpu.make_async_copy(turned.at[pair], out_ref.at[pair], out_sems.at[pair]))
        copies[-1].start()
    for copy in copies:
        copy.wait()


def prev_stay(sides, prev, plan):
    height = prev[0].shape[1]
    return pl.pallas_call(
        prev_stay_kernel,
        out_shape=blocks(PAIRS, height),
        in_specs=specs(pltpu.VMEM, *[pl.ANY] * 3),
        out_specs=pl.BlockSpec(memory_space=pltpu.HBM),
        scratch_shapes=[
            pltpu.VMEM((PAIRS, height, WIDTH), jnp.float32),
            pltpu.SemaphoreType.DMA((PAIRS,)),
            pltpu.VMEM((PLACES, height, WIDTH), jnp.float32),
            pltpu.SemaphoreType.DMA((PLACES,)),
            pltpu.SMEM((1,) + plan.shape, jnp.int32),
            pltpu.SemaphoreType.DMA,
        ],
        compiler_params=PARAMS,
        name="prev_stay",
    )(sides, *prev, plan)


def last_turn_kernel(
    sums_ref, own_stay_ref, own_moved_ref, stay_ref, moved_ref, own_plan_ref, prev_plan_ref,
    out_ref, sides, held, turned, in_sems, out_sems, plan, plan_sems,
):
    plans = load_plans((own_plan_ref, prev_plan_ref), plan, plan_sems)
    for which, refs in enumerate(((own_stay_ref, own_moved_ref), (stay_ref, moved_ref))):
        start_loads([refs[place % 2].at[place // 2] for place in range(PLACES)], held.at[which], in_sems.at[which])
    write_sides(sums_ref, sides)
    for copy in plans:
        copy.wait()
    wait_loads(held.at[0], in_sems.at[0], range(PLACES))
    for copy in turn_all(1, held.at[0], held.at[1], in_sems.at[1], sides, turned, (out_ref,), out_sems, plan):
        copy.wait()


def last_turn(sums, own, prev_stayed, prev_moved, plans):
    height = own[0].shape[1]
    return pl.pallas_call(
        last_turn_kernel,
        out_shape=jax.ShapeDtypeStruct((height, PLACES * WIDTH), jnp.float32),
        in_specs=specs(pltpu.VMEM, *[pltpu.HBM] * 3, *[pl.ANY] * 3),
        out_specs=pl.BlockSpec(memory_space=pltpu.HBM),
        scratch_shapes=[
            pltpu.VMEM((2 * PAIRS, 2 * WIDTH, 2 * WIDTH), jnp.bfloat16),
            pltpu.VMEM((2, PLACES, height, WIDTH), jnp.float32),
            pltpu.VMEM((PLACES, height, WIDTH), jnp.float32),
            pltpu.SemaphoreType.DMA((2, PLACES)),
            pltpu.SemaphoreType.DMA((PLACES,)),
            pltpu.SMEM((2,) + plans[0].shape, jnp.int32),
            pltpu.SemaphoreType.DMA((2,)),
        ],
        compiler_params=PARAMS,
        name="last_turn",
    )(sums, *in_hbm(*own, prev_stayed), prev_moved, *plans)


def onward(value):
    count = lax.axis_size("pairs")
    return lax.ppermute(value, "pairs", [(q, (q + 1) % count) for q in range(count)])


def row_groups():
    return [list(range(start, start + PAIRS)) for start in range(0, lax.axis_size("rows"), PAIRS)]


def summed_mine(parts):
    count = lax.axis_size("rows")
    nx, nz = PAIRS, count // PAIRS
    mine = jnp.sum(lax.all_to_all(parts, "rows", 0, 0, axis_index_groups=row_groups()), axis=0)
    step = 1
    while step < nz:
        turned = nz - 1 if 2 * step == nz else step
        mine = mine + lax.ppermute(mine, "rows", [(i, (((i // nx) ^ turned) * nx) + i % nx) for i in range(count)])
        step *= 2
    return mine


def gathered(mine, theirs):
    both = jnp.stack([mine, theirs])
    return lax.all_to_all(jnp.broadcast_to(both, (PAIRS,) + both.shape), "rows", 0, 0, axis_index_groups=row_groups())


def local(snapshot, plan):
    parts, early, late = first_gram(snapshot, plan)
    prev_early = onward(early)
    mine = summed_mine(parts)
    theirs, prev_plan, sent = lax.optimization_barrier((onward(mine), onward(plan), late))
    prev = (prev_early, onward(sent))
    plans = (plan, prev_plan)
    sides, own = rotate(gathered(mine, theirs), (early, late))
    parts, stay, moved = first_turn(sides, own, prev, plans)
    prev_moved = onward(moved)
    mine = summed_mine(parts)
    theirs = onward(mine)
    prev_stayed = prev_stay(sides, lax.optimization_barrier((prev, mine))[0], prev_plan)
    return last_turn(gathered(mine, theirs), (stay, moved), prev_stayed, prev_moved, plans)


def solution(mesh):
    return jax.shard_map(
        local,
        mesh=mesh,
        in_specs=(P("rows", "pairs"), P(None, "pairs", None)),
        out_specs=P("rows", "pairs"),
        check_vma=False,
    )
```

```python
import functools

import jax
import jax.numpy as jnp
from jax import lax
from jax.experimental import pallas as pl
from jax.experimental.pallas import tpu as pltpu
from jax.sharding import PartitionSpec as P

WIDTH = 128
PAIRS = 4
PLACES = 2 * PAIRS
EARLY = 5
PANEL = 32
PACK = WIDTH // PANEL
SUB = 8
GROUP = 8
GROUP_ROWS = 136
HP = lax.Precision.HIGHEST
PARAMS = pltpu.CompilerParams(vmem_limit_bytes=28 * 1024 * 1024)


def split(value):
    high = value.astype(jnp.bfloat16)
    return high, (value - high.astype(jnp.float32)).astype(jnp.bfloat16)


def home(offset):
    return lax.rem(lax.axis_index("rows") + (PAIRS + offset), PAIRS)


def column_block(array, place):
    return array.at[:, pl.ds(place * WIDTH, WIDTH)]


def gram_pair(first, second, out_ref):
    a, b, c = split3(first)
    d, e, f = split3(second)
    large = contract(jnp.concatenate([a, b], axis=1), jnp.concatenate([d, e], axis=1), 0)
    small = contract(a, f, 0) + contract(c, d, 0)
    middle = large[:WIDTH, WIDTH:] + large[WIDTH:, :WIDTH]
    out_ref[:WIDTH, :] = large[:WIDTH, :WIDTH] + (middle + (large[WIDTH:, WIDTH:] + small))
    line = lax.broadcasted_iota(jnp.int32, (GROUP_ROWS - WIDTH, WIDTH), 0)
    norms = [jnp.sum(block * block, axis=0, keepdims=True) for block in (first, second)]
    out_ref[WIDTH:, :] = jnp.where(line == 0, norms[0], jnp.where(line == 1, norms[1], 0.0))


def first_gram_kernel(plan_ref, x_ref, *refs):
    gram_refs, (early_ref, late_ref, held, sems, out_sems, plan, plan_sem) = refs[:PAIRS], refs[PAIRS:]
    load_plan = pltpu.make_async_copy(plan_ref, plan, plan_sem)
    load_plan.start()
    loads = [
        pltpu.make_async_copy(column_block(x_ref, place), held.at[place], sems.at[place]) for place in range(PLACES)
    ]
    for copy in loads:
        copy.start()
    copies = []
    for place in range(PLACES):
        loads[place].wait()
        target = early_ref.at[place] if place < EARLY else late_ref.at[place - EARLY]
        copies.append(pltpu.make_async_copy(held.at[place], target, out_sems.at[place]))
        copies[-1].start()
    load_plan.wait()
    for offset, gram_ref in enumerate(gram_refs):
        pair = home(offset)
        gram_pair(held[plan[0, 0, 2 * pair]], held[plan[0, 0, 2 * pair + 1]], gram_ref)
    for copy in copies:
        copy.wait()


SUMS = (jax.ShapeDtypeStruct((GROUP_ROWS, WIDTH), jnp.float32),) * PAIRS


def blocks(count, height):
    return pltpu.HBM((count, height, WIDTH), jnp.float32)


def in_hbm(*arrays):
    return tuple(pltpu.with_memory_space_constraint(array, pltpu.HBM) for array in arrays)


def specs(*spaces):
    return [pl.BlockSpec(memory_space=space) for space in spaces]


def first_gram(x, plan):
    height = x.shape[0]
    return pl.pallas_call(
        first_gram_kernel,
        out_shape=SUMS + (blocks(EARLY, height), blocks(PLACES - EARLY, height)),
        in_specs=specs(pltpu.HBM, pltpu.HBM),
        out_specs=specs(*[pltpu.VMEM] * PAIRS, pltpu.HBM, pltpu.HBM),
        scratch_shapes=[
            pltpu.VMEM((PLACES, height, WIDTH), jnp.float32),
            pltpu.SemaphoreType.DMA((PLACES,)),
            pltpu.SemaphoreType.DMA((PLACES,)),
            pltpu.SMEM(plan.shape, jnp.int32),
            pltpu.SemaphoreType.DMA,
        ],
        compiler_params=PARAMS,
        name="first_gram",
    )(*in_hbm(plan, x))


def panel_inverse(block):
    parts = [block[i : i + SUB, :] for i in range(0, PANEL, SUB)]
    row = lax.broadcasted_iota(jnp.int32, (SUB, WIDTH), 0)
    lane = lax.broadcasted_iota(jnp.int32, (SUB, WIDTH), 1)
    base = (lane // PANEL) * PANEL
    inner = lane - base

    def line(value, j):
        return jnp.broadcast_to(value[j // SUB][j % SUB : j % SUB + 1, :], (SUB, WIDTH))

    def column(value, j):
        return [jnp.take_along_axis(part, base + j, axis=1) for part in value]

    for start in range(0, PANEL, GROUP):
        columns = [column(parts, j) for j in range(start, start + GROUP)]
        for j in range(start, start + GROUP, 2):
            c0, c1, *columns = columns
            a, b, d = line(c0, j), line(c1, j), line(c1, j + 1)
            r = 1.0 / (a * d - b * b)

            def update(value, u, v, cleared):
                m0, m1 = (d * u - b * v), (a * v - b * u)
                out = []
                for i in range(len(value)):
                    old = value[i] if cleared is None else jnp.where(cleared, 0.0, value[i])
                    out.append(old - (c0[i] * m0 + c1[i] * m1) * r)
                i = j // SUB
                out[i] = jnp.where(row == j % SUB, m0 * r, jnp.where(row == j % SUB + 1, m1 * r, out[i]))
                return out
            columns = [update(c, line(c, j), line(c, j + 1), None) for c in columns]
            at0, at1 = inner == j, inner == j + 1
            u = jnp.where(at0, 1.0, jnp.where(at1, 0.0, line(parts, j)))
            v = jnp.where(at1, 1.0, jnp.where(at0, 0.0, line(parts, j + 1)))
            parts = update(parts, u, v, at0 | at1)
    return jnp.concatenate(parts, axis=0)


def split3(value):
    high = value.astype(jnp.bfloat16)
    rest = value - high.astype(jnp.float32)
    middle = rest.astype(jnp.bfloat16)
    return high, middle, (rest - middle.astype(jnp.float32)).astype(jnp.bfloat16)


def contract(left, right, over):
    return lax.dot_general(left, right, (((over,), (over,)), ((), ())), preferred_element_type=jnp.float32)


def tall_dot(left, right):
    (a, b, c), (d, e, f) = left, right
    return contract(jnp.concatenate([a, b, a, b, c, a], axis=0), jnp.concatenate([d, d, e, e, d, f], axis=0), 0)


def square_dot(left, right, over):
    (a, b, c), (d, e, f) = left, right
    pair = lambda x, y: jnp.concatenate([x, y], axis=over)
    return contract(pair(a, b), pair(d, e), over) + (
        contract(pair(a, b), pair(e, d), over) + contract(pair(a, c), pair(f, d), over)
    )


def rotations(sums, count):
    width = WIDTH
    row = lax.broadcasted_iota(jnp.int32, (width, width), 0)
    lane = lax.broadcasted_iota(jnp.int32, (width, width), 1)
    eye = (row == lane).astype(jnp.float32)
    halves, systems = [], []
    for pair in range(count):
        cross = sums[pair][:width, :]
        scale = lax.rsqrt(sums[pair][width:, :] + 1e-06)
        down = jnp.sum(eye * scale[0:1, :], axis=1, keepdims=True)
        half = 0.5 * cross * down * scale[1:2, :]
        parts = split3(half)
        spd = eye + square_dot(parts, parts, 1)
        halves.append((half, parts))
        systems.append(jnp.concatenate([spd, half], axis=1))
    group = lax.broadcasted_iota(jnp.int32, (PANEL, width), 1) // PANEL
    wide = lax.broadcasted_iota(jnp.int32, (PANEL, 2 * width), 1)
    wide_row = lax.broadcasted_iota(jnp.int32, (PANEL, 2 * width), 0)
    for panel in range(width // PANEL):
        lo, hi = panel * PANEL, (panel + 1) * PANEL
        inside = (wide >= lo) & (wide < hi)
        cleared = jnp.concatenate([inside] * (width // PANEL), axis=0)
        done = []
        for first in range(0, count, PACK):
            members = range(first, min(first + PACK, count))
            packed = None
            for pair in members:
                part = systems[pair][lo:hi, :width]
                shift = ((pair - first) * PANEL - lo) % width
                if shift:
                    part = pltpu.roll(part, shift, 1)
                packed = part if packed is None else jnp.where(group == pair - first, part, packed)
            inverse = split3(panel_inverse(packed))
            for pair in members:
                old = systems[pair]
                top = old[lo:hi, :]
                unit = jnp.where(inside, (wide - lo == wide_row).astype(jnp.float32), top)
                at = (pair - first) * PANEL
                fresh = tall_dot(inverse, split3(unit))[at : at + PANEL, :]
                side = jnp.where(lane[:PANEL] < lo, -top[:, :width], top[:, :width])
                change = tall_dot(split3(side), split3(fresh))
                updated = jnp.where(cleared, 0.0, old) - change
                done.append(jnp.concatenate(([updated[:lo]] if lo else []) + [fresh] + ([updated[hi:]] if hi < width else []), axis=0))
        systems = done
    return [(halves[pair][0], systems[pair][:, :width], systems[pair][:, width:]) for pair in range(count)]


def write_sides(sums, sides_ref):
    width = WIDTH
    row = lax.broadcasted_iota(jnp.int32, (width, width), 0)
    lane = lax.broadcasted_iota(jnp.int32, (width, width), 1)
    eye = (row == lane).astype(jnp.float32)

    def write(index, top, bottom):
        for start, part in ((0, top), (width, bottom)):
            high, low = split(part)
            sides_ref[index, start : start + width, :width] = high
            sides_ref[index, start : start + width, width:] = low

    for index, (half, inverse, across) in enumerate(rotations(sums, len(sums))):
        pair = home(-(index % PAIRS))
        if index >= PAIRS:
            write(PAIRS + pair, 2.0 * across, eye - 2.0 * square_dot(split3(half), split3(across), 0))
        left = 0 if index < PAIRS else 2 * PAIRS
        if left < sides_ref.shape[0]:
            write(left + pair, 2.0 * inverse - eye, -2.0 * across.T)


def rotate_kernel(*refs):
    sums, (early_ref, late_ref, sides_ref, own_ref, sems) = refs[: 2 * PAIRS], refs[2 * PAIRS :]
    start_loads(sent_blocks(early_ref, late_ref), own_ref, sems)
    write_sides(sums, sides_ref)
    wait_loads(own_ref, sems, range(PLACES))


def rotate(sums, own):
    return pl.pallas_call(
        rotate_kernel,
        out_shape=(
            jax.ShapeDtypeStruct((3 * PAIRS, 2 * WIDTH, 2 * WIDTH), jnp.bfloat16),
            pltpu.VMEM((PLACES, own[0].shape[1], WIDTH), jnp.float32),
        ),
        in_specs=specs(*[pltpu.VMEM] * len(sums), pltpu.HBM, pltpu.HBM),
        out_specs=specs(pltpu.VMEM, pltpu.VMEM),
        scratch_shapes=[pltpu.SemaphoreType.DMA((PLACES,))],
        compiler_params=PARAMS,
        name="rotate",
    )(*sums, *in_hbm(*own))


def turned_pair(held, both, side):
    high, low = split(jnp.concatenate([held[place] for place in both], axis=1))
    parts = jnp.dot(high, side, preferred_element_type=jnp.float32)
    rest = jnp.dot(low, side[:, :WIDTH], preferred_element_type=jnp.float32)
    return parts[:, :WIDTH] + (parts[:, WIDTH:] + rest)


def start_loads(sources, held, sems):
    for place, source in enumerate(sources):
        pltpu.make_async_copy(source, held.at[place], sems.at[place]).start()


def wait_loads(held, sems, both):
    for place in both:
        pltpu.make_async_copy(held.at[0], held.at[place], sems.at[place]).wait()


def load_plans(refs, plan, sems):
    copies = [pltpu.make_async_copy(ref, plan.at[which], sems.at[which]) for which, ref in enumerate(refs)]
    for copy in copies:
        copy.start()
    return copies


def sent_blocks(early_ref, late_ref):
    return [early_ref.at[place] if place < EARLY else late_ref.at[place - EARLY] for place in range(PLACES)]


def both_of(plan, which, step, pair):
    return [plan[which, step, 0, 2 * pair + i] for i in range(2)]


def turn_all(step, own, prev, prev_sems, sides_ref, turned, outs, out_sems, plan):
    copies = []
    for which, held in enumerate((own, prev)):
        for pair in range(PAIRS):
            both = both_of(plan, which, step, pair)
            if which:
                wait_loads(prev, prev_sems, both)
            place = 2 * pair + which
            turned[place] = turned_pair(held, both, sides_ref[which * PAIRS + pair])
            target = column_block(outs[0], place) if len(outs) == 1 else outs[which].at[pair]
            copies.append(pltpu.make_async_copy(turned.at[place], target, out_sems.at[place]))
            copies[-1].start()
    return copies


def first_turn_kernel(
    sides_ref, own_ref, early_ref, late_ref, own_plan_ref, prev_plan_ref,
    *refs,
):
    gram_refs, refs = refs[:PAIRS], refs[PAIRS:]
    stay_ref, moved_ref, held, turned, in_sems, out_sems, plan, plan_sems = refs
    plans = load_plans((own_plan_ref, prev_plan_ref), plan, plan_sems)
    start_loads(sent_blocks(early_ref, late_ref), held, in_sems)
    for copy in plans:
        copy.wait()
    copies = turn_all(0, own_ref, held, in_sems, sides_ref, turned, (stay_ref, moved_ref), out_sems, plan)
    for offset, gram_ref in enumerate(gram_refs):
        first, second = [turned[place] for place in both_of(plan, 0, 1, home(offset))]
        gram_pair(first, second, gram_ref)
    for copy in copies:
        copy.wait()


def first_turn(sides, own, prev, plans):
    height = own.shape[1]
    return pl.pallas_call(
        first_turn_kernel,
        out_shape=SUMS + (blocks(PAIRS, height), blocks(PAIRS, height)),
        in_specs=specs(pltpu.VMEM, pltpu.VMEM, *[pl.ANY] * 4),
        out_specs=specs(*[pltpu.VMEM] * PAIRS, pltpu.HBM, pltpu.HBM),
        scratch_shapes=[
            pltpu.VMEM((PLACES, height, WIDTH), jnp.float32),
            pltpu.VMEM((PLACES, height, WIDTH), jnp.float32),
            pltpu.SemaphoreType.DMA((PLACES,)),
            pltpu.SemaphoreType.DMA((PLACES,)),
            pltpu.SMEM((2,) + plans[0].shape, jnp.int32),
            pltpu.SemaphoreType.DMA((2,)),
        ],
        compiler_params=PARAMS,
        name="first_turn",
    )(sides, own, *prev, *plans)


def prev_stay_kernel(sides_ref, early_ref, late_ref, plan_ref, out_ref, turned, out_sems, held, in_sems, plan, plan_sem):
    load_plan = pltpu.make_async_copy(plan_ref, plan.at[0], plan_sem)
    load_plan.start()
    start_loads(sent_blocks(early_ref, late_ref), held, in_sems)
    load_plan.wait()
    copies = []
    for pair in range(PAIRS):
        both = both_of(plan, 0, 0, pair)
        wait_loads(held, in_sems, both)
        turned[pair] = turned_pair(held, both, sides_ref[2 * PAIRS + pair])
        copies.append(pltpu.make_async_copy(turned.at[pair], out_ref.at[pair], out_sems.at[pair]))
        copies[-1].start()
    for copy in copies:
        copy.wait()


def prev_stay(sides, prev, plan):
    height = prev[0].shape[1]
    return pl.pallas_call(
        prev_stay_kernel,
        out_shape=blocks(PAIRS, height),
        in_specs=specs(pltpu.VMEM, *[pl.ANY] * 3),
        out_specs=pl.BlockSpec(memory_space=pltpu.HBM),
        scratch_shapes=[
            pltpu.VMEM((PAIRS, height, WIDTH), jnp.float32),
            pltpu.SemaphoreType.DMA((PAIRS,)),
            pltpu.VMEM((PLACES, height, WIDTH), jnp.float32),
            pltpu.SemaphoreType.DMA((PLACES,)),
            pltpu.SMEM((1,) + plan.shape, jnp.int32),
            pltpu.SemaphoreType.DMA,
        ],
        compiler_params=PARAMS,
        name="prev_stay",
    )(sides, *prev, plan)


def last_turn_kernel(*refs):
    sums, refs = refs[: 2 * PAIRS], refs[2 * PAIRS :]
    own_stay_ref, own_moved_ref, stay_ref, moved_ref, own_plan_ref, prev_plan_ref, *refs = refs
    out_ref, sides, held, turned, in_sems, out_sems, plan, plan_sems = refs
    plans = load_plans((own_plan_ref, prev_plan_ref), plan, plan_sems)
    for which, refs in enumerate(((own_stay_ref, own_moved_ref), (stay_ref, moved_ref))):
        start_loads([refs[place % 2].at[place // 2] for place in range(PLACES)], held.at[which], in_sems.at[which])
    write_sides(sums, sides)
    for copy in plans:
        copy.wait()
    wait_loads(held.at[0], in_sems.at[0], range(PLACES))
    for copy in turn_all(1, held.at[0], held.at[1], in_sems.at[1], sides, turned, (out_ref,), out_sems, plan):
        copy.wait()


def last_turn(sums, own, prev_stayed, prev_moved, plans):
    height = own[0].shape[1]
    return pl.pallas_call(
        last_turn_kernel,
        out_shape=jax.ShapeDtypeStruct((height, PLACES * WIDTH), jnp.float32),
        in_specs=specs(*[pltpu.VMEM] * len(sums), *[pltpu.HBM] * 3, *[pl.ANY] * 3),
        out_specs=pl.BlockSpec(memory_space=pltpu.HBM),
        scratch_shapes=[
            pltpu.VMEM((2 * PAIRS, 2 * WIDTH, 2 * WIDTH), jnp.bfloat16),
            pltpu.VMEM((2, PLACES, height, WIDTH), jnp.float32),
            pltpu.VMEM((PLACES, height, WIDTH), jnp.float32),
            pltpu.SemaphoreType.DMA((2, PLACES)),
            pltpu.SemaphoreType.DMA((PLACES,)),
            pltpu.SMEM((2,) + plans[0].shape, jnp.int32),
            pltpu.SemaphoreType.DMA((2,)),
        ],
        compiler_params=PARAMS,
        name="last_turn",
    )(*sums, *in_hbm(*own, prev_stayed), prev_moved, *plans)


def onward(value):
    count = lax.axis_size("pairs")
    return lax.ppermute(value, "pairs", [(q, (q + 1) % count) for q in range(count)])


def along_rows(value, target):
    count = lax.axis_size("rows")
    return lax.ppermute(value, "rows", [(i, target(i // PAIRS, i % PAIRS)) for i in range(count)])


def along_x(value, offset):
    return along_rows(value, lambda z, x: z * PAIRS + (x + offset) % PAIRS)


def summed_mine(parts):
    nz = lax.axis_size("rows") // PAIRS
    first, second, third, fourth = [along_x(part, offset) if offset else part for offset, part in enumerate(parts)]
    mine = (first + second) + (third + fourth)
    step = 1
    while step < nz:
        turned = nz - 1 if 2 * step == nz else step
        mine = mine + along_rows(mine, lambda z, x: (z ^ turned) * PAIRS + x)
        step *= 2
    return mine


def gathered(value):
    return [along_x(value, offset) if offset else value for offset in range(PAIRS)]


def local(snapshot, plan):
    *parts, early, late = first_gram(snapshot, plan)
    prev_early = onward(early)
    mine = summed_mine(parts)
    theirs, prev_plan, sent = lax.optimization_barrier((onward(mine), onward(plan), late))
    prev = (prev_early, onward(sent))
    plans = (plan, prev_plan)
    sides, own = rotate(gathered(mine) + gathered(theirs), (early, late))
    *parts, stay, moved = first_turn(sides, own, prev, plans)
    prev_moved = onward(moved)
    mine = summed_mine(parts)
    theirs = onward(mine)
    prev_stayed = prev_stay(sides, lax.optimization_barrier((prev, mine))[0], prev_plan)
    return last_turn(gathered(mine) + gathered(theirs), (stay, moved), prev_stayed, prev_moved, plans)


def solution(mesh):
    return jax.shard_map(
        local,
        mesh=mesh,
        in_specs=(P("rows", "pairs"), P(None, "pairs", None)),
        out_specs=P("rows", "pairs"),
        check_vma=False,
    )
```

```python
import functools

import jax
import jax.numpy as jnp
from jax import lax
from jax.experimental import pallas as pl
from jax.experimental.pallas import tpu as pltpu
from jax.sharding import PartitionSpec as P

WIDTH = 128
PAIRS = 4
PLACES = 2 * PAIRS
EARLY = 5
PANEL = 32
PACK = WIDTH // PANEL
SUB = 8
GROUP = 8
GROUP_ROWS = 136
HP = lax.Precision.HIGHEST
PARAMS = pltpu.CompilerParams(vmem_limit_bytes=28 * 1024 * 1024)


def split(value):
    high = value.astype(jnp.bfloat16)
    return high, (value - high.astype(jnp.float32)).astype(jnp.bfloat16)


def home(offset):
    return lax.rem(lax.axis_index("rows") + (PAIRS + offset), PAIRS)


def column_block(array, place):
    return array.at[:, pl.ds(place * WIDTH, WIDTH)]


def gram_pair(first, second, out_ref):
    a, b, c = split3(first)
    d, e, f = split3(second)
    large = contract(jnp.concatenate([a, b], axis=1), jnp.concatenate([d, e], axis=1), 0)
    small = contract(a, f, 0) + contract(c, d, 0)
    middle = large[:WIDTH, WIDTH:] + large[WIDTH:, :WIDTH]
    out_ref[:WIDTH, :] = large[:WIDTH, :WIDTH] + (middle + (large[WIDTH:, WIDTH:] + small))
    line = lax.broadcasted_iota(jnp.int32, (GROUP_ROWS - WIDTH, WIDTH), 0)
    norms = [jnp.sum(block * block, axis=0, keepdims=True) for block in (first, second)]
    out_ref[WIDTH:, :] = jnp.where(line == 0, norms[0], jnp.where(line == 1, norms[1], 0.0))


def first_gram_kernel(plan_ref, x_ref, *refs):
    gram_refs, (early_ref, late_ref, held, sems, out_sems, plan, plan_sem) = refs[:PAIRS], refs[PAIRS:]
    load_plan = pltpu.make_async_copy(plan_ref, plan, plan_sem)
    load_plan.start()
    loads = [
        pltpu.make_async_copy(column_block(x_ref, place), held.at[place], sems.at[place]) for place in range(PLACES)
    ]
    for copy in loads:
        copy.start()
    copies = []
    for place in range(PLACES):
        loads[place].wait()
        target = early_ref.at[place] if place < EARLY else late_ref.at[place - EARLY]
        copies.append(pltpu.make_async_copy(held.at[place], target, out_sems.at[place]))
        copies[-1].start()
    load_plan.wait()
    for offset, gram_ref in enumerate(gram_refs):
        pair = home(offset)
        gram_pair(held[plan[0, 0, 2 * pair]], held[plan[0, 0, 2 * pair + 1]], gram_ref)
    for copy in copies:
        copy.wait()


SUMS = (jax.ShapeDtypeStruct((GROUP_ROWS, WIDTH), jnp.float32),) * PAIRS


def blocks(count, height):
    return pltpu.HBM((count, height, WIDTH), jnp.float32)


def in_hbm(*arrays):
    return tuple(pltpu.with_memory_space_constraint(array, pltpu.HBM) for array in arrays)


def specs(*spaces):
    return [pl.BlockSpec(memory_space=space) for space in spaces]


def first_gram(x, plan):
    height = x.shape[0]
    return pl.pallas_call(
        first_gram_kernel,
        out_shape=SUMS + (blocks(EARLY, height), blocks(PLACES - EARLY, height)),
        in_specs=specs(pltpu.HBM, pltpu.HBM),
        out_specs=specs(*[pltpu.VMEM] * PAIRS, pltpu.HBM, pltpu.HBM),
        scratch_shapes=[
            pltpu.VMEM((PLACES, height, WIDTH), jnp.float32),
            pltpu.SemaphoreType.DMA((PLACES,)),
            pltpu.SemaphoreType.DMA((PLACES,)),
            pltpu.SMEM(plan.shape, jnp.int32),
            pltpu.SemaphoreType.DMA,
        ],
        compiler_params=PARAMS,
        name="first_gram",
    )(*in_hbm(plan, x))


def panel_inverse(block):
    parts = [block[i : i + SUB, :] for i in range(0, PANEL, SUB)]
    row = lax.broadcasted_iota(jnp.int32, (SUB, WIDTH), 0)
    lane = lax.broadcasted_iota(jnp.int32, (SUB, WIDTH), 1)
    base = (lane // PANEL) * PANEL
    inner = lane - base

    def line(value, j):
        return jnp.broadcast_to(value[j // SUB][j % SUB : j % SUB + 1, :], (SUB, WIDTH))

    def column(value, j):
        return [jnp.take_along_axis(part, base + j, axis=1) for part in value]

    for start in range(0, PANEL, GROUP):
        columns = [column(parts, j) for j in range(start, start + GROUP)]
        for j in range(start, start + GROUP, 2):
            c0, c1, *columns = columns
            a, b, d = line(c0, j), line(c1, j), line(c1, j + 1)
            r = 1.0 / (a * d - b * b)

            def update(value, u, v, cleared):
                m0, m1 = (d * u - b * v), (a * v - b * u)
                out = []
                for i in range(len(value)):
                    old = value[i] if cleared is None else jnp.where(cleared, 0.0, value[i])
                    out.append(old - (c0[i] * m0 + c1[i] * m1) * r)
                i = j // SUB
                out[i] = jnp.where(row == j % SUB, m0 * r, jnp.where(row == j % SUB + 1, m1 * r, out[i]))
                return out
            columns = [update(c, line(c, j), line(c, j + 1), None) for c in columns]
            at0, at1 = inner == j, inner == j + 1
            u = jnp.where(at0, 1.0, jnp.where(at1, 0.0, line(parts, j)))
            v = jnp.where(at1, 1.0, jnp.where(at0, 0.0, line(parts, j + 1)))
            parts = update(parts, u, v, at0 | at1)
    return jnp.concatenate(parts, axis=0)


def split3(value):
    high = value.astype(jnp.bfloat16)
    rest = value - high.astype(jnp.float32)
    middle = rest.astype(jnp.bfloat16)
    return high, middle, (rest - middle.astype(jnp.float32)).astype(jnp.bfloat16)


def contract(left, right, over):
    return lax.dot_general(left, right, (((over,), (over,)), ((), ())), preferred_element_type=jnp.float32)


def tall_dot(left, right):
    (a, b, c), (d, e, f) = left, right
    return contract(jnp.concatenate([a, b, a, b, c, a], axis=0), jnp.concatenate([d, d, e, e, d, f], axis=0), 0)


def square_dot(left, right, over):
    (a, b, c), (d, e, f) = left, right
    pair = lambda x, y: jnp.concatenate([x, y], axis=over)
    return contract(pair(a, b), pair(d, e), over) + (
        contract(pair(a, b), pair(e, d), over) + contract(pair(a, c), pair(f, d), over)
    )


def rotations(sums, count):
    width = WIDTH
    row = lax.broadcasted_iota(jnp.int32, (width, width), 0)
    lane = lax.broadcasted_iota(jnp.int32, (width, width), 1)
    eye = (row == lane).astype(jnp.float32)
    halves, systems = [], []
    for pair in range(count):
        cross = sums[pair][:width, :]
        scale = lax.rsqrt(sums[pair][width:, :] + 1e-06)
        down = jnp.sum(eye * scale[0:1, :], axis=1, keepdims=True)
        half = 0.5 * cross * down * scale[1:2, :]
        parts = split3(half)
        spd = eye + square_dot(parts, parts, 1)
        halves.append((half, parts))
        systems.append(jnp.concatenate([spd, half], axis=1))
    group = lax.broadcasted_iota(jnp.int32, (PANEL, width), 1) // PANEL
    wide = lax.broadcasted_iota(jnp.int32, (PANEL, 2 * width), 1)
    wide_row = lax.broadcasted_iota(jnp.int32, (PANEL, 2 * width), 0)
    for panel in range(width // PANEL):
        lo, hi = panel * PANEL, (panel + 1) * PANEL
        inside = (wide >= lo) & (wide < hi)
        cleared = jnp.concatenate([inside] * (width // PANEL), axis=0)
        done = []
        for first in range(0, count, PACK):
            members = range(first, min(first + PACK, count))
            packed = None
            for pair in members:
                part = systems[pair][lo:hi, :width]
                shift = ((pair - first) * PANEL - lo) % width
                if shift:
                    part = pltpu.roll(part, shift, 1)
                packed = part if packed is None else jnp.where(group == pair - first, part, packed)
            inverse = split3(panel_inverse(packed))
            for pair in members:
                old = systems[pair]
                top = old[lo:hi, :]
                unit = jnp.where(inside, (wide - lo == wide_row).astype(jnp.float32), top)
                at = (pair - first) * PANEL
                fresh = tall_dot(inverse, split3(unit))[at : at + PANEL, :]
                side = jnp.where(lane[:PANEL] < lo, -top[:, :width], top[:, :width])
                change = tall_dot(split3(side), split3(fresh))
                updated = jnp.where(cleared, 0.0, old) - change
                done.append(jnp.concatenate(([updated[:lo]] if lo else []) + [fresh] + ([updated[hi:]] if hi < width else []), axis=0))
        systems = done
    return [(halves[pair][0], systems[pair][:, :width], systems[pair][:, width:]) for pair in range(count)]


def write_sides(sums, sides_ref, relative):
    width = WIDTH
    row = lax.broadcasted_iota(jnp.int32, (width, width), 0)
    lane = lax.broadcasted_iota(jnp.int32, (width, width), 1)
    eye = (row == lane).astype(jnp.float32)

    def write(index, top, bottom):
        for start, part in ((0, top), (width, bottom)):
            high, low = split(part)
            sides_ref[index, start : start + width, :width] = high
            sides_ref[index, start : start + width, width:] = low

    for index, (half, inverse, across) in enumerate(rotations(sums, len(sums))):
        pair = home(-(index % PAIRS)) if relative else index % PAIRS
        if index >= PAIRS:
            write(PAIRS + pair, 2.0 * across, eye - 2.0 * square_dot(split3(half), split3(across), 0))
        left = 0 if index < PAIRS else 2 * PAIRS
        if left < sides_ref.shape[0]:
            write(left + pair, 2.0 * inverse - eye, -2.0 * across.T)


def rotate_kernel(sums_ref, early_ref, late_ref, sides_ref, own_ref, sems):
    sums = [sums_ref.at[pair, which] for which in range(2) for pair in range(PAIRS)]
    start_loads(sent_blocks(early_ref, late_ref), own_ref, sems)
    write_sides(sums, sides_ref, False)
    wait_loads(own_ref, sems, range(PLACES))


def rotate(sums, own):
    return pl.pallas_call(
        rotate_kernel,
        out_shape=(
            jax.ShapeDtypeStruct((3 * PAIRS, 2 * WIDTH, 2 * WIDTH), jnp.bfloat16),
            pltpu.VMEM((PLACES, own[0].shape[1], WIDTH), jnp.float32),
        ),
        in_specs=specs(pltpu.VMEM, pltpu.HBM, pltpu.HBM),
        out_specs=specs(pltpu.VMEM, pltpu.VMEM),
        scratch_shapes=[pltpu.SemaphoreType.DMA((PLACES,))],
        compiler_params=PARAMS,
        name="rotate",
    )(sums, *in_hbm(*own))


def turned_pair(held, both, side):
    high, low = split(jnp.concatenate([held[place] for place in both], axis=1))
    parts = jnp.dot(high, side, preferred_element_type=jnp.float32)
    rest = jnp.dot(low, side[:, :WIDTH], preferred_element_type=jnp.float32)
    return parts[:, :WIDTH] + (parts[:, WIDTH:] + rest)


def start_loads(sources, held, sems):
    for place, source in enumerate(sources):
        pltpu.make_async_copy(source, held.at[place], sems.at[place]).start()


def wait_loads(held, sems, both):
    for place in both:
        pltpu.make_async_copy(held.at[0], held.at[place], sems.at[place]).wait()


def load_plans(refs, plan, sems):
    copies = [pltpu.make_async_copy(ref, plan.at[which], sems.at[which]) for which, ref in enumerate(refs)]
    for copy in copies:
        copy.start()
    return copies


def sent_blocks(early_ref, late_ref):
    return [early_ref.at[place] if place < EARLY else late_ref.at[place - EARLY] for place in range(PLACES)]


def both_of(plan, which, step, pair):
    return [plan[which, step, 0, 2 * pair + i] for i in range(2)]


def turn_all(step, own, prev, prev_sems, sides_ref, turned, outs, out_sems, plan):
    copies = []
    for which, held in enumerate((own, prev)):
        for pair in range(PAIRS):
            both = both_of(plan, which, step, pair)
            if which:
                wait_loads(prev, prev_sems, both)
            place = 2 * pair + which
            turned[place] = turned_pair(held, both, sides_ref[which * PAIRS + pair])
            target = column_block(outs[0], place) if len(outs) == 1 else outs[which].at[pair]
            copies.append(pltpu.make_async_copy(turned.at[place], target, out_sems.at[place]))
            copies[-1].start()
    return copies


def first_turn_kernel(
    sides_ref, own_ref, early_ref, late_ref, own_plan_ref, prev_plan_ref,
    *refs,
):
    gram_refs, refs = refs[:PAIRS], refs[PAIRS:]
    stay_ref, moved_ref, held, turned, in_sems, out_sems, plan, plan_sems = refs
    plans = load_plans((own_plan_ref, prev_plan_ref), plan, plan_sems)
    start_loads(sent_blocks(early_ref, late_ref), held, in_sems)
    for copy in plans:
        copy.wait()
    copies = turn_all(0, own_ref, held, in_sems, sides_ref, turned, (stay_ref, moved_ref), out_sems, plan)
    for offset, gram_ref in enumerate(gram_refs):
        first, second = [turned[place] for place in both_of(plan, 0, 1, home(offset))]
        gram_pair(first, second, gram_ref)
    for copy in copies:
        copy.wait()


def first_turn(sides, own, prev, plans):
    height = own.shape[1]
    return pl.pallas_call(
        first_turn_kernel,
        out_shape=SUMS + (blocks(PAIRS, height), blocks(PAIRS, height)),
        in_specs=specs(pltpu.VMEM, pltpu.VMEM, *[pl.ANY] * 4),
        out_specs=specs(*[pltpu.VMEM] * PAIRS, pltpu.HBM, pltpu.HBM),
        scratch_shapes=[
            pltpu.VMEM((PLACES, height, WIDTH), jnp.float32),
            pltpu.VMEM((PLACES, height, WIDTH), jnp.float32),
            pltpu.SemaphoreType.DMA((PLACES,)),
            pltpu.SemaphoreType.DMA((PLACES,)),
            pltpu.SMEM((2,) + plans[0].shape, jnp.int32),
            pltpu.SemaphoreType.DMA((2,)),
        ],
        compiler_params=PARAMS,
        name="first_turn",
    )(sides, own, *prev, *plans)


def prev_stay_kernel(sides_ref, early_ref, late_ref, plan_ref, out_ref, turned, out_sems, held, in_sems, plan, plan_sem):
    load_plan = pltpu.make_async_copy(plan_ref, plan.at[0], plan_sem)
    load_plan.start()
    start_loads(sent_blocks(early_ref, late_ref), held, in_sems)
    load_plan.wait()
    copies = []
    for pair in range(PAIRS):
        both = both_of(plan, 0, 0, pair)
        wait_loads(held, in_sems, both)
        turned[pair] = turned_pair(held, both, sides_ref[2 * PAIRS + pair])
        copies.append(pltpu.make_async_copy(turned.at[pair], out_ref.at[pair], out_sems.at[pair]))
        copies[-1].start()
    for copy in copies:
        copy.wait()


def prev_stay(sides, prev, plan):
    height = prev[0].shape[1]
    return pl.pallas_call(
        prev_stay_kernel,
        out_shape=blocks(PAIRS, height),
        in_specs=specs(pltpu.VMEM, *[pl.ANY] * 3),
        out_specs=pl.BlockSpec(memory_space=pltpu.HBM),
        scratch_shapes=[
            pltpu.VMEM((PAIRS, height, WIDTH), jnp.float32),
            pltpu.SemaphoreType.DMA((PAIRS,)),
            pltpu.VMEM((PLACES, height, WIDTH), jnp.float32),
            pltpu.SemaphoreType.DMA((PLACES,)),
            pltpu.SMEM((1,) + plan.shape, jnp.int32),
            pltpu.SemaphoreType.DMA,
        ],
        compiler_params=PARAMS,
        name="prev_stay",
    )(sides, *prev, plan)


def last_turn_kernel(*refs):
    sums, refs = refs[: 2 * PAIRS], refs[2 * PAIRS :]
    own_stay_ref, own_moved_ref, stay_ref, moved_ref, own_plan_ref, prev_plan_ref, *refs = refs
    out_ref, sides, held, turned, in_sems, out_sems, plan, plan_sems = refs
    plans = load_plans((own_plan_ref, prev_plan_ref), plan, plan_sems)
    for which, refs in enumerate(((own_stay_ref, own_moved_ref), (stay_ref, moved_ref))):
        start_loads([refs[place % 2].at[place // 2] for place in range(PLACES)], held.at[which], in_sems.at[which])
    write_sides(sums, sides, True)
    for copy in plans:
        copy.wait()
    wait_loads(held.at[0], in_sems.at[0], range(PLACES))
    for copy in turn_all(1, held.at[0], held.at[1], in_sems.at[1], sides, turned, (out_ref,), out_sems, plan):
        copy.wait()


def last_turn(sums, own, prev_stayed, prev_moved, plans):
    height = own[0].shape[1]
    return pl.pallas_call(
        last_turn_kernel,
        out_shape=jax.ShapeDtypeStruct((height, PLACES * WIDTH), jnp.float32),
        in_specs=specs(*[pltpu.VMEM] * len(sums), *[pltpu.HBM] * 3, *[pl.ANY] * 3),
        out_specs=pl.BlockSpec(memory_space=pltpu.HBM),
        scratch_shapes=[
            pltpu.VMEM((2 * PAIRS, 2 * WIDTH, 2 * WIDTH), jnp.bfloat16),
            pltpu.VMEM((2, PLACES, height, WIDTH), jnp.float32),
            pltpu.VMEM((PLACES, height, WIDTH), jnp.float32),
            pltpu.SemaphoreType.DMA((2, PLACES)),
            pltpu.SemaphoreType.DMA((PLACES,)),
            pltpu.SMEM((2,) + plans[0].shape, jnp.int32),
            pltpu.SemaphoreType.DMA((2,)),
        ],
        compiler_params=PARAMS,
        name="last_turn",
    )(*sums, *in_hbm(*own, prev_stayed), prev_moved, *plans)


def onward(value):
    count = lax.axis_size("pairs")
    return lax.ppermute(value, "pairs", [(q, (q + 1) % count) for q in range(count)])


def along_rows(value, target):
    count = lax.axis_size("rows")
    return lax.ppermute(value, "rows", [(i, target(i // PAIRS, i % PAIRS)) for i in range(count)])


def along_x(value, offset):
    return along_rows(value, lambda z, x: z * PAIRS + (x + offset) % PAIRS)


def summed_mine(parts):
    nz = lax.axis_size("rows") // PAIRS
    first, second, third, fourth = [along_x(part, offset) if offset else part for offset, part in enumerate(parts)]
    mine = (first + second) + (third + fourth)
    step = 1
    while step < nz:
        turned = nz - 1 if 2 * step == nz else step
        mine = mine + along_rows(mine, lambda z, x: (z ^ turned) * PAIRS + x)
        step *= 2
    return mine


def gathered(value):
    return [along_x(value, offset) if offset else value for offset in range(PAIRS)]


def gathered_both(mine, theirs):
    both = jnp.stack([mine, theirs])
    beside = [list(range(start, start + PAIRS)) for start in range(0, lax.axis_size("rows"), PAIRS)]
    return lax.all_to_all(jnp.broadcast_to(both, (PAIRS,) + both.shape), "rows", 0, 0, axis_index_groups=beside)


def local(snapshot, plan):
    *parts, early, late = first_gram(snapshot, plan)
    prev_early = onward(early)
    mine = summed_mine(parts)
    theirs, prev_plan, sent = lax.optimization_barrier((onward(mine), onward(plan), late))
    prev = (prev_early, onward(sent))
    plans = (plan, prev_plan)
    sides, own = rotate(gathered_both(mine, theirs), (early, late))
    *parts, stay, moved = first_turn(sides, own, prev, plans)
    prev_moved = onward(moved)
    mine = summed_mine(parts)
    theirs = onward(mine)
    prev_stayed = prev_stay(sides, lax.optimization_barrier((prev, mine))[0], prev_plan)
    return last_turn(gathered(mine) + gathered(theirs), (stay, moved), prev_stayed, prev_moved, plans)


def solution(mesh):
    return jax.shard_map(
        local,
        mesh=mesh,
        in_specs=(P("rows", "pairs"), P(None, "pairs", None)),
        out_specs=P("rows", "pairs"),
        check_vma=False,
    )
```
